128 devices in a mesh: grp: 2 (over core), dev: 64 (over z, x, y).
Axes of the slice: x: 4, y: 4, z: 4, core: 2. Of those that a mesh axis runs over, the one named last changes fastest.
Arguments:
- source_emb: bfloat16 [64, 786432], P(None, ('grp', 'dev'))
- target_emb: bfloat16 [64, 786432], P(None, ('grp', 'dev'))
- target_pot: bfloat16 [786432], P(('grp', 'dev')), may hold values from -5 to 5
- log_src: float32 [786432], P(('grp', 'dev')), may hold values from -1 to 1
- log_tgt: float32 [786432], P(('grp', 'dev')), may hold values from -1 to 1
- pair_list: int32 [2304, 2], replicated, may hold values from 0 to 767, as said below
Outputs:
- source_potential: float32 [786432], P(('grp', 'dev'))
- target_potential: float32 [786432], P(('grp', 'dev'))
The draws below stay inside these ranges and needn't reach their ends.
Inputs may be any that keep to these rules, and one draw needn't show every extreme that they name: `pair_list`: rows are distinct (source block, target block) pairs sorted by source block. Device d (numbered over grp then dev) owns blocks d * 6 to (d + 1) * 6 - 1 of each side. Every block of each side appears in some row. A row's target block is owned by the owner of its source block or by a device next to it. The rows before the first row of device d's source blocks number d * 18 + e_d, where e_0 = 0, e_1 = 3 and 1 <= e_d <= 3 for d >= 2; so rows k * 18 to (k + 1) * 18 - 1 have source blocks owned by devices k - 1 and k, and the source blocks of one device appear in 15 to 21 rows, exactly 21 for device 0.
All inputs are finite; a program needn't handle non-finite values.
Results may differ from the reference program's by a relative error of at most 0.0005.
Values may be sent and summed in bfloat16 or wider, within the bound.
No kernel may reach another device: no remote copies, remote signals or barrier semaphores. Data moves between devices by JAX's collectives and lax.ppermute only.
A program may use at most 256 MiB of HBM per device.

```python
import jax
import jax.numpy as jnp
from jax import lax

W = 64
BLK = 1024
SB_DEV = 6
P_DEV = 18
NB = 768
NS = 786432
NPAIRS = 2304


def draw_source_emb(key, part):
    key = jax.random.fold_in(key, 3)
    normal_part = 0.25 * jax.random.normal(key, (W, NS), jnp.float32)
    return normal_part.astype(jnp.bfloat16)


def draw_target_emb(key, part):
    key = jax.random.fold_in(key, 5)
    normal_part = 0.25 * jax.random.normal(key, (W, NS), jnp.float32)
    return normal_part.astype(jnp.bfloat16)


def draw_pair_list(key, part):
    key = jax.random.fold_in(key, 11)
    devices = NB // SB_DEV
    half_block = SB_DEV // 2
    key_dev, key_grid, key_order = jax.random.split(key, 3)
    device_ids = jnp.arange(devices, dtype=jnp.int32)
    amounts = jax.random.randint(key_dev, (devices,), 1, half_block + 1).astype(jnp.int32)
    amounts = amounts.at[1].set(half_block)
    offsets = jnp.where(device_ids == 0, 0, amounts).astype(jnp.int32)
    offsets_next = jnp.concatenate([offsets[1:], jnp.zeros((1,), jnp.int32)])
    totals = (P_DEV + offsets_next - offsets).astype(jnp.int32)
    per_block = 3 * SB_DEV - 1
    grid_cells = SB_DEV * per_block
    at_edge = (device_ids == 0) | (device_ids == devices - 1)
    usable_slots = jnp.where(at_edge, 2 * SB_DEV - 1, per_block)
    slot_of_cell = jnp.arange(grid_cells, dtype=jnp.int32) % per_block
    cell_usable = slot_of_cell[None, :] < usable_slots[:, None]
    grid_keys = jax.random.split(key_grid, devices)
    rank_grid = jax.vmap(lambda subkey: jax.random.permutation(subkey, grid_cells))(grid_keys).astype(jnp.int32)
    grid_scores = jnp.where(cell_usable, rank_grid, grid_cells + rank_grid)
    grid_order = jnp.argsort(grid_scores, axis=1, stable=True)
    grid_place = jnp.argsort(grid_order, axis=1, stable=True).astype(jnp.int32)
    chosen = (grid_place < (totals - SB_DEV)[:, None]).astype(jnp.int32)
    counts = (1 + chosen.reshape(devices, SB_DEV, per_block).sum(axis=2)).reshape(NB)
    block_ids = jnp.arange(NB, dtype=jnp.int32)
    owner_dev = block_ids // SB_DEV
    low_block = (owner_dev - 1) * SB_DEV
    span_size = 3 * SB_DEV
    order_keys = jax.random.split(key_order, NB)
    rank_rows = jax.vmap(lambda subkey: jax.random.permutation(subkey, span_size))(order_keys).astype(jnp.int32)
    candidate = jnp.arange(span_size, dtype=jnp.int32)
    candidate_block = low_block[:, None] + candidate[None, :]
    inside = (candidate_block >= 0) & (candidate_block < NB)
    scores = jnp.where(inside, rank_rows, span_size + rank_rows)
    scores = jnp.where(candidate[None, :] == (block_ids - low_block)[:, None], -1, scores)
    target_order = jnp.argsort(scores, axis=1, stable=True).astype(jnp.int32)
    starts = (jnp.cumsum(counts) - counts).astype(jnp.int32)
    row_ids = jnp.arange(NPAIRS, dtype=jnp.int32)
    source = (jnp.searchsorted(starts, row_ids, side='right') - 1).astype(jnp.int32)
    slot_ids = row_ids - starts[source]
    target = low_block[source] + target_order[source, slot_ids]
    return jnp.stack([source, target], axis=1).astype(jnp.int32)


def block_levels(rng, dims, shards, low, high):
    gain = 1.0
    for position, blocks in shards:
        draws = jax.random.uniform(jax.random.fold_in(jax.random.fold_in(rng, 6), position), (blocks,), jnp.float32, low / len(shards), high / len(shards))
        gain = gain * jnp.repeat(jnp.exp(draws), dims[position] // blocks).reshape((-1,) + (1,) * (len(dims) - 1 - position))
    return gain


def noise(own_key, extent, width, most, cuts=(), kind=jnp.bfloat16):
    result = jax.random.normal(own_key, extent, jnp.float32) * width
    if len(cuts) > 0:
        result = block_levels(own_key, extent, cuts, -0.22, 0.18) * result
    return jnp.clip(result, min=-most, max=most).astype(kind)


def setup_inputs(seed: int = 0) -> dict:
    seeds = jax.random.split(jax.random.key(seed), 7)
    return {
        "source_emb": draw_source_emb(jax.random.fold_in(seeds[6], 71), 0),
        "target_emb": draw_target_emb(jax.random.fold_in(seeds[6], 71), 0),
        "target_pot": noise(seeds[2], (NS,), 1.0, 5.0, ((0, 128),)),
        "log_src": jnp.clip(jax.random.uniform(seeds[3], (NS,), jnp.float32, -1.0, 1.0) * block_levels(seeds[3], (NS,), ((0, 128),), -0.4, 0.0), -1.0, 1.0),
        "log_tgt": jnp.clip(jax.random.uniform(seeds[4], (NS,), jnp.float32, -1.0, 1.0) * block_levels(seeds[4], (NS,), ((0, 128),), -0.4, 0.0), -1.0, 1.0),
        "pair_list": draw_pair_list(jax.random.fold_in(seeds[6], 71), 0),
    }


blur_scale = 0.5
floor_value = -1.0e30


def tile_cost(source_tile, target_tile):
    source_full = source_tile.astype(jnp.float32)
    target_full = target_tile.astype(jnp.float32)
    source_norm = jnp.sum(source_full * source_full, axis=0)
    target_norm = jnp.sum(target_full * target_full, axis=0)
    inner_term = lax.dot_general(source_tile, target_tile, (((0,), (0,)), ((), ())), preferred_element_type=jnp.float32)
    return 0.5 * source_norm[:, None] + 0.5 * target_norm[None, :] - inner_term


def combine(first_max, first_sum, second_max, second_sum):
    shared_max = jnp.maximum(first_max, second_max)
    return shared_max, first_sum * jnp.exp(first_max - shared_max) + second_sum * jnp.exp(second_max - shared_max)


def reference(source_emb, target_emb, target_pot, log_src, log_tgt, pair_list):
    cell_count = source_emb.shape[1]
    initial = (jnp.full((cell_count,), floor_value, jnp.float32), jnp.zeros((cell_count,), jnp.float32))

    def row_step(running, block_pair):
        row_max, row_sum = running
        src_place = block_pair[0] * BLK
        tgt_place = block_pair[1] * BLK
        source_tile = lax.dynamic_slice_in_dim(source_emb, src_place, BLK, 1)
        target_tile = lax.dynamic_slice_in_dim(target_emb, tgt_place, BLK, 1)
        target_here = lax.dynamic_slice_in_dim(target_pot, tgt_place, BLK, 0).astype(jnp.float32)
        logits = (target_here[None, :] - tile_cost(source_tile, target_tile)) / blur_scale
        tile_max = jnp.max(logits, axis=1)
        tile_sum = jnp.sum(jnp.exp(logits - tile_max[:, None]), axis=1)
        old_max = lax.dynamic_slice_in_dim(row_max, src_place, BLK, 0)
        old_sum = lax.dynamic_slice_in_dim(row_sum, src_place, BLK, 0)
        new_max, new_sum = combine(old_max, old_sum, tile_max, tile_sum)
        row_max = lax.dynamic_update_slice_in_dim(row_max, new_max, src_place, 0)
        row_sum = lax.dynamic_update_slice_in_dim(row_sum, new_sum, src_place, 0)
        return (row_max, row_sum), None

    (row_max, row_sum), unused = lax.scan(row_step, initial, pair_list)
    source_potential = blur_scale * (log_src - (row_max + jnp.log(row_sum)))

    def col_step(running, block_pair):
        col_max, col_sum = running
        src_place = block_pair[0] * BLK
        tgt_place = block_pair[1] * BLK
        source_tile = lax.dynamic_slice_in_dim(source_emb, src_place, BLK, 1)
        target_tile = lax.dynamic_slice_in_dim(target_emb, tgt_place, BLK, 1)
        source_here = lax.dynamic_slice_in_dim(source_potential, src_place, BLK, 0)
        logits = (source_here[:, None] - tile_cost(source_tile, target_tile)) / blur_scale
        tile_max = jnp.max(logits, axis=0)
        tile_sum = jnp.sum(jnp.exp(logits - tile_max[None, :]), axis=0)
        old_max = lax.dynamic_slice_in_dim(col_max, tgt_place, BLK, 0)
        old_sum = lax.dynamic_slice_in_dim(col_sum, tgt_place, BLK, 0)
        new_max, new_sum = combine(old_max, old_sum, tile_max, tile_sum)
        col_max = lax.dynamic_update_slice_in_dim(col_max, new_max, tgt_place, 0)
        col_sum = lax.dynamic_update_slice_in_dim(col_sum, new_sum, tgt_place, 0)
        return (col_max, col_sum), None

    (col_max, col_sum), unused = lax.scan(col_step, initial, pair_list)
    target_potential = blur_scale * (log_tgt - (col_max + jnp.log(col_sum)))
    return source_potential, target_potential
```

```python
import functools

import jax
import jax.numpy as jnp
from jax import lax
from jax.experimental import pallas as pl
from jax.experimental.pallas import tpu as pltpu
from jax.sharding import PartitionSpec as P

BLK = 1024
P_DEV = 18
W = 64
DEPTH = 80
MOST = 21
KEEP_OWN = 11
KEEP_LEFT = 5
KEEP_RIGHT = 5
FLOOR = -1.0e30
SPAN = 75.0
ROWS = 256
AXES = ("grp", "dev")
f32 = jnp.float32
bf16 = jnp.bfloat16


def shifted(value, steps):
    count = lax.axis_size(AXES)
    first, last = max(0, -steps), min(count, count - steps)
    return lax.ppermute(value, AXES, [(i, i + steps) for i in range(first, last)])


def place(meta, p):
    device = meta[0]
    blocks = meta[1]
    source = meta[2 + p] - device * blocks
    target = meta[2 + MOST + p] - device * blocks
    valid = (source >= 0) & (source < blocks)
    side = jnp.where(target < 0, -1, jnp.where(target >= blocks, 1, 0))
    return valid, jnp.clip(source, 0, blocks - 1), side, target - side * blocks


def list_rows(meta, side_wanted, rows):
    def step(p, count):
        valid, _, side, _ = place(meta, p)
        take = valid & (side == side_wanted)

        @pl.when(take)
        def _():
            rows[count] = p

        return count + take.astype(jnp.int32)

    return lax.fori_loop(0, MOST, step, jnp.int32(0))


def cells(block):
    return pl.ds(pl.multiple_of(block * BLK, BLK), BLK)


def fill_targets(y, c, ya):
    for t in range(ya.shape[0]):
        ya[t, 0:W, :] = y[:, t * BLK : (t + 1) * BLK]
        row = c[:, t * BLK : (t + 1) * BLK]
        high = row.astype(bf16).astype(f32)
        rest = row - high
        middle = rest.astype(bf16).astype(f32)
        low = rest - middle
        index = lax.broadcasted_iota(jnp.int32, (DEPTH - W, BLK), 0)
        extra = jnp.where(
            index == 0, high, jnp.where(index == 1, middle, jnp.where(index == 2, low, 0.0))
        )
        ya[t, W:DEPTH, :] = extra.astype(bf16)


def kernel_values(xt, ya, s, t, sums, keep, slot):
    for first in range(0, BLK, ROWS):
        here = pl.ds(first, ROWS)
        k = jnp.exp(jnp.dot(xt[s, here, :], ya[t], preferred_element_type=f32))
        if sums is not None:
            part = k[:, 0:128]
            for j in range(128, BLK, 128):
                part = part + k[:, j : j + 128]
            sums[s, here, :] += part
        if keep is not None:
            keep[slot, here, :] = k.astype(bf16)


def row_pairs(meta, rows, count, xt, ya, sums, keep, capacity):
    @pl.loop(0, jnp.minimum(count, capacity))
    def _(n):
        _, s, _, t = place(meta, rows[n])
        kernel_values(xt, ya, s, t, sums, keep, n)

    @pl.loop(jnp.minimum(count, capacity), count)
    def _(n):
        _, s, _, t = place(meta, rows[n])
        kernel_values(xt, ya, s, t, sums, None, 0)


def column_pairs(meta, rows, count, xt, ya, u, keep, capacity, spare, spare_slot, totals, base):
    def add(s, t, k):
        totals[base + t] += jnp.dot(u[s].astype(bf16), k, preferred_element_type=f32)

    @pl.loop(0, jnp.minimum(count, capacity))
    def _(n):
        _, s, _, t = place(meta, rows[n])
        add(s, t, keep[n])

    @pl.loop(jnp.minimum(count, capacity), count)
    def _(n):
        _, s, _, t = place(meta, rows[n])
        kernel_values(xt, ya, s, t, None, spare, spare_slot)
        add(s, t, spare[spare_slot])


def norms(x, s):
    full = x[:, s * BLK : (s + 1) * BLK].astype(f32)
    return jnp.sum(full * full, axis=0, keepdims=True)


def logs(total):
    return jnp.where(total > 0.0, jnp.log(jnp.where(total > 0.0, total, 1.0)), FLOOR)


STEP = 128


def fetch(meta, p, ys, cs, y_block, c_block):
    _, _, side, t = place(meta, p)
    for side_here, y, c in zip((-1, 0, 1), ys, cs):
        if y is None:
            continue

        @pl.when(side == side_here)
        def _():
            y_block[...] = y[:, cells(t)]
            c_block[...] = c[:, cells(t)]


def products(x, s, first, y_block):
    x_part = x[:, pl.ds(pl.multiple_of(s * BLK + first, STEP), STEP)]
    return 2.0 * lax.dot_general(
        x_part, y_block[...], (((0,), (0,)), ((), ())), preferred_element_type=f32
    )


def general_rows(meta, x, ys, cs, y_block, c_block, top, mass, log_rows):
    @pl.loop(0, MOST)
    def _(p):
        valid, s, _, _ = place(meta, p)
        before_valid, before, _, _ = place(meta, jnp.maximum(p - 1, 0))

        @pl.when(valid)
        def _():
            @pl.when((p == 0) | jnp.logical_not(before_valid) | (before != s))
            def _():
                top[...] = jnp.full_like(top, FLOOR)
                mass[...] = jnp.zeros_like(mass)

            fetch(meta, p, ys, cs, y_block, c_block)

            @pl.loop(0, BLK // STEP)
            def _(q):
                here = pl.ds(pl.multiple_of(q * STEP, STEP), STEP)
                logits = products(x, s, q * STEP, y_block) + c_block[...]
                old = top[here, :]
                new = jnp.maximum(old, jnp.max(logits, axis=1, keepdims=True))
                terms = jnp.sum(jnp.exp(logits - new[:, 0:1]), axis=1, keepdims=True)
                mass[here, :] = mass[here, :] * jnp.exp(old - new) + terms
                top[here, :] = new

            log_rows[:, cells(s)] = jnp.transpose(top[...] + jnp.log(mass[...]))[0:1, :]


def general_columns(meta, sides, base, x, ys, cs, y_block, c_block, weight, column, col_top, col_mass):
    @pl.loop(0, MOST)
    def _(p):
        valid, s, side, t = place(meta, p)
        wanted = side == sides[0]
        for other in sides[1:]:
            wanted = wanted | (side == other)

        @pl.when(valid & wanted)
        def _():
            fetch(meta, p, ys, cs, y_block, c_block)
            column[...] = jnp.transpose(jnp.broadcast_to(weight[:, cells(s)], (128, BLK)))
            slot = base(side, t)

            @pl.loop(0, BLK // STEP)
            def _(q):
                here = pl.ds(pl.multiple_of(q * STEP, STEP), STEP)
                logits = products(x, s, q * STEP, y_block) + c_block[...] + column[here, 0:1]
                old = col_top[slot]
                new = jnp.maximum(old, jnp.max(logits, axis=0, keepdims=True))
                terms = jnp.sum(jnp.exp(logits - new[0:1, :]), axis=0, keepdims=True)
                col_mass[slot] = col_mass[slot] * jnp.exp(old - new) + terms
                col_top[slot] = new


def own_rows_kernel(meta, x, y, c, xt, keep, sums, rows, ya):
    blocks = sums.shape[0]
    for s in range(blocks):
        doubled = 2.0 * x[:, s * BLK : (s + 1) * BLK].astype(f32)
        xt[s, :, 0:W] = jnp.transpose(doubled).astype(bf16)
        xt[s, :, W:DEPTH] = jnp.ones((BLK, DEPTH - W), bf16)
    fill_targets(y, c, ya)
    sums[...] = jnp.zeros_like(sums)
    count = list_rows(meta, 0, rows)
    row_pairs(meta, rows, count, xt, ya, sums, keep, KEEP_OWN)


def left_rows_kernel(meta, xt, y, c, before, keep, sums, rows, ya):
    fill_targets(y, c, ya)
    sums[...] = before[...]
    count = list_rows(meta, -1, rows)
    row_pairs(meta, rows, count, xt, ya, sums, keep, KEEP_LEFT)


def settle_kernel(
    meta, xt, x, y_left, c_left, y_own, c_own, y_right, c_right, before, keep_left, log_src,
    potential, send_left, send_right, u, weight, fits,
    rows_left, rows_right, ya_left, ya_right, keep, sums, totals,
    y_block, c_block, top, mass, column, col_top, col_mass,
):
    blocks = u.shape[0]
    fill_targets(y_left, c_left, ya_left)
    fill_targets(y_right, c_right, ya_right)
    sums[...] = before[...]
    count_left = list_rows(meta, -1, rows_left)
    count_right = list_rows(meta, 1, rows_right)
    row_pairs(meta, rows_right, count_right, xt, ya_right, sums, keep, KEEP_RIGHT)

    largest = norms(x, 0)
    for s in range(1, blocks):
        largest = jnp.maximum(largest, norms(x, s))
    lowest = jnp.minimum(jnp.minimum(c_left[...], c_right[...]), c_own[...])
    x2 = jnp.max(largest, axis=1, keepdims=True)
    c_min = jnp.min(lowest, axis=1, keepdims=True)
    y2 = jnp.maximum(10.0 - c_min, 0.0)
    extent = x2 + 10.0 + 2.0 * jnp.sqrt(x2) * jnp.sqrt(y2) - c_min
    in_range = jnp.max(extent) <= SPAN
    fits[...] = jnp.broadcast_to(jnp.where(extent <= SPAN, 1.0, 0.0), fits.shape)
    offset = lambda side, t: jnp.where(side < 0, t, blocks + t)

    @pl.when(in_range)
    def _():
        index = lax.broadcasted_iota(jnp.int32, (8, BLK), 0)
        for s in range(blocks):
            here = slice(s * BLK, (s + 1) * BLK)
            total = jnp.sum(jnp.transpose(sums[s]), axis=0, keepdims=True)
            w = log_src[:, here] - jnp.log(total)
            weight[:, here] = w
            value = jnp.exp(w)
            high = value.astype(bf16).astype(f32)
            u[s] = jnp.where(index == 0, high, jnp.where(index == 1, value - high, 0.0))
        totals[...] = jnp.zeros_like(totals)
        column_pairs(
            meta, rows_left, count_left, xt, ya_left, u, keep_left, KEEP_LEFT,
            keep, KEEP_RIGHT, totals, 0,
        )
        column_pairs(
            meta, rows_right, count_right, xt, ya_right, u, keep, KEEP_RIGHT,
            keep, KEEP_RIGHT, totals, blocks,
        )
        for t in range(blocks):
            here = slice(t * BLK, (t + 1) * BLK)
            send_left[:, here] = logs(jnp.sum(totals[t], axis=0, keepdims=True))
            send_right[:, here] = logs(jnp.sum(totals[blocks + t], axis=0, keepdims=True))

    @pl.when(jnp.logical_not(in_range))
    def _():
        ys = (y_left, y_own, y_right)
        cs = (c_left, c_own, c_right)
        general_rows(meta, x, ys, cs, y_block, c_block, top, mass, weight)
        weight[...] = log_src[...] - weight[...]
        u[...] = jnp.zeros_like(u)
        col_top[...] = jnp.full_like(col_top, FLOOR)
        col_mass[...] = jnp.zeros_like(col_mass)
        general_columns(
            meta, (-1, 1), offset, x, ys, cs, y_block, c_block, weight, column, col_top, col_mass
        )
        for t in range(blocks):
            here = slice(t * BLK, (t + 1) * BLK)
            send_left[:, here] = (col_top[t] + logs(col_mass[t]))[0:1, :]
            send_right[:, here] = (col_top[blocks + t] + logs(col_mass[blocks + t]))[0:1, :]

    for s in range(blocks):
        here = slice(s * BLK, (s + 1) * BLK)
        potential[:, here] = 0.5 * (weight[:, here] + norms(x, s))


def own_columns_kernel(
    meta, xt, x, y, c, keep, u, weight, fits,
    out,
    rows, ya, spare, totals, y_block, c_block, column, col_top, col_mass,
):
    blocks = u.shape[0]
    in_range = jnp.max(fits[...]) > 0.5
    count = list_rows(meta, 0, rows)

    @pl.when(in_range)
    def _():
        @pl.when(count > KEEP_OWN)
        def _():
            fill_targets(y, c, ya)

        totals[...] = jnp.zeros_like(totals)
        column_pairs(meta, rows, count, xt, ya, u, keep, KEEP_OWN, spare, 0, totals, 0)
        for t in range(blocks):
            out[:, t * BLK : (t + 1) * BLK] = logs(jnp.sum(totals[t], axis=0, keepdims=True))

    @pl.when(jnp.logical_not(in_range))
    def _():
        col_top[...] = jnp.full_like(col_top, FLOOR)
        col_mass[...] = jnp.zeros_like(col_mass)
        general_columns(
            meta, (0,), lambda side, t: t, x, (None, y, None), (None, c, None),
            y_block, c_block, weight, column, col_top, col_mass,
        )
        for t in range(blocks):
            here = slice(t * BLK, (t + 1) * BLK)
            out[:, here] = (col_top[t] + logs(col_mass[t]))[0:1, :]


def call(kernel, operands, outs, scratch, limit, pairs):
    in_vmem = pl.BlockSpec(memory_space=pltpu.VMEM)
    in_smem = pl.BlockSpec(memory_space=pltpu.SMEM)
    return pl.pallas_call(
        kernel,
        out_shape=outs,
        in_specs=[in_smem] + [in_vmem] * (len(operands) - 1),
        out_specs=jax.tree.map(lambda _: in_vmem, outs),
        scratch_shapes=scratch,
        compiler_params=pltpu.CompilerParams(vmem_limit_bytes=limit << 20),
        cost_estimate=pl.CostEstimate(
            flops=pairs * 2 * BLK * BLK * 256, bytes_accessed=1 << 20, transcendentals=pairs * BLK * BLK
        ),
    )(*operands)


def on_device(source_emb, target_emb, target_pot, log_src, log_tgt, pair_list):
    position = lax.axis_index(AXES)
    count = lax.axis_size(AXES)
    width = source_emb.shape[1]
    blocks = width // BLK
    row = jax.ShapeDtypeStruct((1, width), f32)
    from_left = shifted(target_emb, 1)
    from_right = shifted(target_emb, -1)

    twice = 2.0 * target_pot.astype(f32)
    full = target_emb.astype(f32)
    c_own = (twice - jnp.sum(full * full, axis=0)).reshape(1, width)
    c_left = shifted(c_own, 1)
    c_right = shifted(c_own, -1)

    mine = lax.dynamic_slice_in_dim(pair_list, position * P_DEV, MOST, 0)
    meta = jnp.concatenate(
        [jnp.stack([position, jnp.int32(blocks)]).astype(jnp.int32), mine[:, 0], mine[:, 1]]
    )

    def kept(n):
        return pltpu.VMEM((n, BLK, BLK), bf16)

    sums_shape = (blocks, BLK, 128)
    ya_shape = pltpu.VMEM((blocks, DEPTH, BLK), bf16)
    rows_shape = pltpu.SMEM((MOST,), jnp.int32)
    xt, keep_own, sums = call(
        own_rows_kernel,
        (meta, source_emb, target_emb, c_own),
        (pltpu.VMEM((blocks, BLK, DEPTH), bf16), kept(KEEP_OWN), pltpu.VMEM(sums_shape, f32)),
        [rows_shape, ya_shape],
        10,
        9,
    )
    keep_left, sums = call(
        left_rows_kernel,
        (meta, xt, from_left, c_left, sums),
        (kept(KEEP_LEFT), pltpu.VMEM(sums_shape, f32)),
        [rows_shape, ya_shape],
        10,
        4,
    )
    block_scratch = [pltpu.VMEM((W, BLK), bf16), pltpu.VMEM((1, BLK), f32)]
    wide = pltpu.VMEM((BLK, 128), f32)
    potential, send_left, send_right, u, weight, fits = call(
        settle_kernel,
        (meta, xt, source_emb, from_left, c_left, target_emb, c_own, from_right, c_right,
         sums, keep_left, log_src.reshape(1, width)),
        (row, row, row, pltpu.VMEM((blocks, 8, BLK), f32), row, jax.ShapeDtypeStruct((1, 128), f32)),
        [rows_shape, rows_shape, ya_shape, ya_shape, kept(KEEP_RIGHT + 1), pltpu.VMEM(sums_shape, f32),
         pltpu.VMEM((2 * blocks, 8, BLK), f32)] + block_scratch + [wide, wide, wide]
        + [pltpu.VMEM((2 * blocks, 1, BLK), f32)] * 2,
        25,
        8,
    )
    got_right = shifted(send_left, -1)
    got_left = shifted(send_right, 1)
    own = call(
        own_columns_kernel,
        (meta, xt, source_emb, target_emb, c_own, keep_own, u, weight, fits),
        row,
        [rows_shape, ya_shape, kept(1), pltpu.VMEM((blocks, 8, BLK), f32)] + block_scratch + [wide]
        + [pltpu.VMEM((blocks, 1, BLK), f32)] * 2,
        10,
        6,
    )
    got_left = jnp.where(position > 0, got_left, FLOOR)
    got_right = jnp.where(position < count - 1, got_right, FLOOR)
    top = jnp.maximum(jnp.maximum(own, got_left), got_right)
    total = jnp.exp(own - top) + jnp.exp(got_left - top) + jnp.exp(got_right - top)
    target_potential = 0.5 * (log_tgt + twice - (top + jnp.log(total)).reshape(width))
    return potential.reshape(width), target_potential


def solution(mesh):
    return jax.shard_map(
        on_device,
        mesh=mesh,
        in_specs=(P(None, AXES), P(None, AXES), P(AXES), P(AXES), P(AXES), P()),
        out_specs=(P(AXES), P(AXES)),
        check_vma=False,
    )
```

```python
import functools

import jax
import jax.numpy as jnp
from jax import lax
from jax.experimental import pallas as pl
from jax.experimental.pallas import tpu as pltpu
from jax.sharding import PartitionSpec as P

BLK = 1024
P_DEV = 18
W = 64
DEPTH = 80
MOST = 21
KEEP_OWN = 11
KEEP_LEFT = 5
KEEP_RIGHT = 4
FLOOR = -1.0e30
SPAN = 75.0
ROWS = 256
LIMITS = (8, 4, 18, 8)
AXES = ("grp", "dev")
f32 = jnp.float32
bf16 = jnp.bfloat16


def shifted(value, steps):
    count = lax.axis_size(AXES)
    first, last = max(0, -steps), min(count, count - steps)
    return lax.ppermute(value, AXES, [(i, i + steps) for i in range(first, last)])


def place(meta, p):
    device = meta[0]
    blocks = meta[1]
    source = meta[3 + p] - device * blocks
    target = meta[3 + MOST + p] - device * blocks
    valid = (source >= 0) & (source < blocks)
    side = jnp.where(target < 0, -1, jnp.where(target >= blocks, 1, 0))
    return valid, jnp.clip(source, 0, blocks - 1), side, target - side * blocks


def list_rows(meta, side_wanted, rows):
    def step(p, count):
        valid, _, side, _ = place(meta, p)
        take = valid & (side == side_wanted)

        @pl.when(take)
        def _():
            rows[count] = p

        return count + take.astype(jnp.int32)

    return lax.fori_loop(0, MOST, step, jnp.int32(0))


def cells(block):
    return pl.ds(pl.multiple_of(block * BLK, BLK), BLK)


def two_at_a_time(start, stop, body):
    half = lax.shift_right_logical(stop - start, jnp.int32(1))

    @pl.loop(0, half)
    def _(n):
        body(start + 2 * n)
        body(start + 2 * n + 1)

    @pl.when(start + 2 * half < stop)
    def _():
        body(stop - 1)


def fill_offsets(y, c):
    width = c.shape[1]
    pots = y[:, width : width + 128].astype(f32)
    for t in range(width // BLK):
        rows = range(t * (BLK // 128), (t + 1) * (BLK // 128))
        row = jnp.concatenate([pots[r : r + 1, :] for r in rows], axis=1)
        c[:, t * BLK : (t + 1) * BLK] = 2.0 * row - norms(y, t)


def fill_targets(y, c, ya):
    for t in range(ya.shape[0]):
        ya[t, 0:W, :] = y[:, t * BLK : (t + 1) * BLK]
    fill_rows(c, ya)


def refill_targets(y, c, ya):
    for t in range(ya.shape[0]):
        pltpu.sync_copy(y.at[:, pl.ds(t * BLK, BLK)], ya.at[t, pl.ds(0, W), :])
    fill_rows(c, ya)


def fill_rows(c, ya):
    for t in range(ya.shape[0]):
        row = c[:, t * BLK : (t + 1) * BLK]
        high = row.astype(bf16).astype(f32)
        rest = row - high
        middle = rest.astype(bf16).astype(f32)
        low = rest - middle
        index = lax.broadcasted_iota(jnp.int32, (DEPTH - W, BLK), 0)
        extra = jnp.where(
            index == 0, high, jnp.where(index == 1, middle, jnp.where(index == 2, low, 0.0))
        )
        ya[t, W:DEPTH, :] = extra.astype(bf16)


def kernel_values(xt, ya, s, t, sums, keep, slot):
    for first in range(0, BLK, ROWS):
        here = pl.ds(first, ROWS)
        k = jnp.exp(jnp.dot(xt[s, here, :], ya[t], preferred_element_type=f32))
        if sums is not None:
            part = k[:, 0:128]
            for j in range(128, BLK, 128):
                part = part + k[:, j : j + 128]
            sums[s, here, :] += part
        if keep is not None:
            keep[slot, here, :] = k.astype(bf16)


def row_pairs(meta, rows, count, xt, ya, sums, keep, capacity):
    def kept(n):
        _, s, _, t = place(meta, rows[n])
        kernel_values(xt, ya, s, t, sums, keep, n)

    two_at_a_time(0, jnp.minimum(count, capacity), kept)

    @pl.loop(jnp.minimum(count, capacity), count)
    def _(n):
        _, s, _, t = place(meta, rows[n])
        kernel_values(xt, ya, s, t, sums, None, 0)


def column_pairs(meta, rows, count, xt, ya, u, keep, capacity, spare, spare_slot, totals, base):
    def add(s, t, k):
        totals[base + t] += jnp.dot(u[s].astype(bf16), k, preferred_element_type=f32)

    def kept(n):
        _, s, _, t = place(meta, rows[n])
        add(s, t, keep[n])

    two_at_a_time(0, jnp.minimum(count, capacity), kept)

    @pl.loop(jnp.minimum(count, capacity), count)
    def _(n):
        _, s, _, t = place(meta, rows[n])
        kernel_values(xt, ya, s, t, None, spare, spare_slot)
        add(s, t, spare[spare_slot])


def lane_sums(part):
    return jnp.sum(jnp.transpose(part), axis=0, keepdims=True)


def norms(x, s):
    full = x[:, s * BLK : (s + 1) * BLK].astype(f32)
    return jnp.sum(full * full, axis=0, keepdims=True)


def logs(total):
    return jnp.where(total > 0.0, jnp.log(jnp.where(total > 0.0, total, 1.0)), FLOOR)


STEP = 128


def fetch(meta, p, x, ys, cs, x_block, y_block, c_block):
    _, s, side, t = place(meta, p)
    pltpu.sync_copy(x.at[:, cells(s)], x_block)
    for side_here, y, c in zip((-1, 0, 1), ys, cs):
        if y is None:
            continue

        @pl.when(side == side_here)
        def _():
            pltpu.sync_copy(y.at[:, cells(t)], y_block)
            c_block[...] = c[:, cells(t)]


def products(x_block, first, y_block):
    x_part = x_block[:, pl.ds(pl.multiple_of(first, STEP), STEP)]
    return 2.0 * lax.dot_general(
        x_part, y_block[...], (((0,), (0,)), ((), ())), preferred_element_type=f32
    )


def general_rows(meta, x, ys, cs, x_block, y_block, c_block, top, mass, log_rows):
    @pl.loop(0, MOST)
    def _(p):
        valid, s, _, _ = place(meta, p)
        before_valid, before, _, _ = place(meta, jnp.maximum(p - 1, 0))

        @pl.when(valid)
        def _():
            @pl.when((p == 0) | jnp.logical_not(before_valid) | (before != s))
            def _():
                top[...] = jnp.full_like(top, FLOOR)
                mass[...] = jnp.zeros_like(mass)

            fetch(meta, p, x, ys, cs, x_block, y_block, c_block)

            @pl.loop(0, BLK // STEP)
            def _(q):
                here = pl.ds(pl.multiple_of(q * STEP, STEP), STEP)
                logits = products(x_block, q * STEP, y_block) + c_block[...]
                old = top[here, :]
                new = jnp.maximum(old, jnp.max(logits, axis=1, keepdims=True))
                terms = jnp.sum(jnp.exp(logits - new[:, 0:1]), axis=1, keepdims=True)
                mass[here, :] = mass[here, :] * jnp.exp(old - new) + terms
                top[here, :] = new

            log_rows[:, cells(s)] = jnp.transpose(top[...] + jnp.log(mass[...]))[0:1, :]


def general_columns(
    meta, sides, base, x, ys, cs, x_block, y_block, c_block, weight, column, col_top, col_mass
):
    @pl.loop(0, MOST)
    def _(p):
        valid, s, side, t = place(meta, p)
        wanted = side == sides[0]
        for other in sides[1:]:
            wanted = wanted | (side == other)

        @pl.when(valid & wanted)
        def _():
            fetch(meta, p, x, ys, cs, x_block, y_block, c_block)
            column[...] = jnp.transpose(jnp.broadcast_to(weight[:, cells(s)], (128, BLK)))
            slot = base(side, t)

            @pl.loop(0, BLK // STEP)
            def _(q):
                here = pl.ds(pl.multiple_of(q * STEP, STEP), STEP)
                logits = products(x_block, q * STEP, y_block) + c_block[...] + column[here, 0:1]
                old = col_top[slot]
                new = jnp.maximum(old, jnp.max(logits, axis=0, keepdims=True))
                terms = jnp.sum(jnp.exp(logits - new[0:1, :]), axis=0, keepdims=True)
                col_mass[slot] = col_mass[slot] * jnp.exp(old - new) + terms
                col_top[slot] = new


def own_rows_kernel(meta, x, y, xt, keep, total, c, norm, rows, ya, sums):
    blocks = sums.shape[0]
    for s in range(blocks):
        norm[:, s * BLK : (s + 1) * BLK] = norms(x, s)
        doubled = 2.0 * x[:, s * BLK : (s + 1) * BLK].astype(f32)
        xt[s, :, 0:W] = jnp.transpose(doubled).astype(bf16)
        xt[s, :, W:DEPTH] = jnp.ones((BLK, DEPTH - W), bf16)
    fill_offsets(y, c)
    fill_targets(y, c, ya)
    sums[...] = jnp.zeros_like(sums)
    count = list_rows(meta, 0, rows)
    row_pairs(meta, rows, count, xt, ya, sums, keep, KEEP_OWN)
    for s in range(blocks):
        total[:, s * BLK : (s + 1) * BLK] = lane_sums(sums[s])


def left_rows_kernel(meta, xt, y, keep, sums, c, rows, ya):
    fill_offsets(y, c)
    fill_targets(y, c, ya)
    sums[...] = jnp.zeros_like(sums)
    count = list_rows(meta, -1, rows)
    row_pairs(meta, rows, count, xt, ya, sums, keep, KEEP_LEFT)


def settle_kernel(
    meta, xt, x, y_left, c_left, y_own, c_own, y_right, norm, own_total, left_sums, keep_left, log_src,
    potential, send_left, send_right, u, weight, fits, no_left, no_right,
    rows_left, rows_right, c_right, ya, keep, sums, totals,
    x_block, y_block, c_block, col_top, col_mass,
):
    blocks = u.shape[0]
    top, mass, column = sums.at[0], sums.at[1], sums.at[2]
    fill_offsets(y_right, c_right)
    fill_targets(y_right, c_right, ya)
    sums[...] = jnp.zeros_like(sums)
    count_left = list_rows(meta, -1, rows_left)
    count_right = list_rows(meta, 1, rows_right)
    row_pairs(meta, rows_right, count_right, xt, ya, sums, keep, KEEP_RIGHT)

    lowest = jnp.minimum(jnp.minimum(c_left[...], c_right[...]), c_own[...])
    x2 = jnp.max(norm[...], axis=1, keepdims=True)
    c_min = jnp.min(lowest, axis=1, keepdims=True)
    y2 = jnp.maximum(10.0 - c_min, 0.0)
    extent = x2 + 10.0 + 2.0 * jnp.sqrt(x2) * jnp.sqrt(y2) - c_min
    in_range = jnp.max(extent) <= SPAN
    no_left[...] = jnp.full_like(no_left, jnp.where(meta[0] == 0, FLOOR, 0.0))
    no_right[...] = jnp.full_like(no_right, jnp.where(meta[0] == meta[2] - 1, FLOOR, 0.0))
    fits[...] = jnp.broadcast_to(jnp.where(extent <= SPAN, 1.0, 0.0), fits.shape)
    offset = lambda side, t: jnp.where(side < 0, t, blocks + t)

    @pl.when(in_range)
    def _():
        index = lax.broadcasted_iota(jnp.int32, (8, BLK), 0)
        for s in range(blocks):
            here = slice(s * BLK, (s + 1) * BLK)
            total = own_total[:, here] + lane_sums(left_sums[s] + sums[s])
            w = log_src[:, here] - jnp.log(total)
            weight[:, here] = w
            value = jnp.exp(w)
            high = value.astype(bf16).astype(f32)
            u[s] = jnp.where(index == 0, high, jnp.where(index == 1, value - high, 0.0))
        totals[...] = jnp.zeros_like(totals)
        column_pairs(
            meta, rows_right, count_right, xt, ya, u, keep, KEEP_RIGHT,
            keep, KEEP_RIGHT, totals, blocks,
        )

        @pl.when(count_left > KEEP_LEFT)
        def _():
            refill_targets(y_left, c_left, ya)

        column_pairs(
            meta, rows_left, count_left, xt, ya, u, keep_left, KEEP_LEFT,
            keep, KEEP_RIGHT, totals, 0,
        )
        for t in range(blocks):
            here = slice(t * BLK, (t + 1) * BLK)
            send_left[:, here] = logs(jnp.sum(totals[t], axis=0, keepdims=True))
            send_right[:, here] = logs(jnp.sum(totals[blocks + t], axis=0, keepdims=True))

    @pl.when(jnp.logical_not(in_range))
    def _():
        ys = (y_left, y_own, y_right)
        cs = (c_left, c_own, c_right)
        general_rows(meta, x, ys, cs, x_block, y_block, c_block, top, mass, weight)
        weight[...] = log_src[...] - weight[...]
        u[...] = jnp.zeros_like(u)
        col_top[...] = jnp.full_like(col_top, FLOOR)
        col_mass[...] = jnp.zeros_like(col_mass)
        general_columns(
            meta, (-1, 1), offset, x, ys, cs, x_block, y_block, c_block, weight, column,
            col_top, col_mass,
        )
        for t in range(blocks):
            here = slice(t * BLK, (t + 1) * BLK)
            send_left[:, here] = (col_top[t] + logs(col_mass[t]))[0:1, :]
            send_right[:, here] = (col_top[blocks + t] + logs(col_mass[blocks + t]))[0:1, :]

    potential[...] = 0.5 * (weight[...] + norm[...])


def own_columns_kernel(
    meta, xt, x, y, c, keep, u, weight, fits,
    out,
    rows, ya, spare, totals, x_block, y_block, c_block, column, col_top, col_mass,
):
    blocks = u.shape[0]
    in_range = jnp.max(fits[...]) > 0.5
    count = list_rows(meta, 0, rows)

    @pl.when(in_range)
    def _():
        @pl.when(count > KEEP_OWN)
        def _():
            refill_targets(y, c, ya)

        totals[...] = jnp.zeros_like(totals)
        column_pairs(meta, rows, count, xt, ya, u, keep, KEEP_OWN, spare, 0, totals, 0)
        for t in range(blocks):
            out[:, t * BLK : (t + 1) * BLK] = logs(jnp.sum(totals[t], axis=0, keepdims=True))

    @pl.when(jnp.logical_not(in_range))
    def _():
        col_top[...] = jnp.full_like(col_top, FLOOR)
        col_mass[...] = jnp.zeros_like(col_mass)
        general_columns(
            meta, (0,), lambda side, t: t, x, (None, y, None), (None, c, None),
            x_block, y_block, c_block, weight, column, col_top, col_mass,
        )
        for t in range(blocks):
            here = slice(t * BLK, (t + 1) * BLK)
            out[:, here] = (col_top[t] + logs(col_mass[t]))[0:1, :]


def call(kernel, operands, outs, scratch, limit, pairs, outside=()):
    in_vmem = pl.BlockSpec(memory_space=pltpu.VMEM)
    in_smem = pl.BlockSpec(memory_space=pltpu.SMEM)
    anywhere = pl.BlockSpec(memory_space=pl.ANY)
    return pl.pallas_call(
        kernel,
        out_shape=outs,
        in_specs=[in_smem]
        + [anywhere if n in outside else in_vmem for n in range(1, len(operands))],
        out_specs=jax.tree.map(lambda _: in_vmem, outs),
        scratch_shapes=scratch,
        compiler_params=pltpu.CompilerParams(vmem_limit_bytes=limit << 20),
        cost_estimate=pl.CostEstimate(
            flops=pairs * 2 * BLK * BLK * 256, bytes_accessed=1 << 20, transcendentals=pairs * BLK * BLK
        ),
    )(*operands)


def on_device(source_emb, target_emb, target_pot, log_src, log_tgt, pair_list):
    position = lax.axis_index(AXES)
    width = source_emb.shape[1]
    blocks = width // BLK
    row = jax.ShapeDtypeStruct((1, width), f32)
    pots = target_pot.reshape(width // 128, 128)
    pots = jnp.pad(pots, ((0, W - width // 128), (0, 0)))
    packed = jnp.concatenate([target_emb, pots], axis=1)
    from_left = shifted(packed, 1)
    from_right = shifted(packed, -1)
    twice = 2.0 * target_pot.astype(f32)

    mine = lax.dynamic_slice_in_dim(pair_list, position * P_DEV, MOST, 0)
    meta = jnp.concatenate(
        [jnp.stack([position, jnp.int32(blocks), jnp.int32(lax.axis_size(AXES))]).astype(jnp.int32), mine[:, 0], mine[:, 1]]
    )

    def kept(n):
        return pltpu.VMEM((n, BLK, BLK), bf16)

    sums_shape = (blocks, BLK, 128)
    ya_shape = pltpu.VMEM((blocks, DEPTH, BLK), bf16)
    rows_shape = pltpu.SMEM((MOST,), jnp.int32)
    row_here = pltpu.VMEM((1, width), f32)
    xt, keep_own, own_total, c_own, norm = call(
        own_rows_kernel,
        (meta, source_emb, packed),
        (pltpu.VMEM((blocks, BLK, DEPTH), bf16), kept(KEEP_OWN), row_here, row_here, row_here),
        [rows_shape, ya_shape, pltpu.VMEM(sums_shape, f32)],
        LIMITS[0],
        9,
    )
    keep_left, left_sums, c_left = call(
        left_rows_kernel,
        (meta, xt, from_left),
        (kept(KEEP_LEFT), pltpu.VMEM(sums_shape, f32), row_here),
        [rows_shape, ya_shape],
        LIMITS[1],
        4,
    )
    block_scratch = [pltpu.VMEM((W, BLK), bf16)] * 2 + [pltpu.VMEM((1, BLK), f32)]
    wide = pltpu.VMEM((BLK, 128), f32)
    one = jax.ShapeDtypeStruct((1, 128), f32)
    potential, send_left, send_right, u, weight, fits, no_left, no_right = call(
        settle_kernel,
        (meta, xt, source_emb, from_left, c_left, target_emb, c_own, from_right, norm,
         own_total, left_sums, keep_left, log_src.reshape(1, width)),
        (row, row, row, pltpu.VMEM((blocks, 8, BLK), f32), row, one, one, one),
        [rows_shape, rows_shape, row_here, ya_shape, kept(KEEP_RIGHT + 1),
         pltpu.VMEM(sums_shape, f32), pltpu.VMEM((2 * blocks, 8, BLK), f32)] + block_scratch
        + [pltpu.VMEM((2 * blocks, 1, BLK), f32)] * 2,
        LIMITS[2],
        8,
        (2, 3, 5),
    )
    got_left = shifted(send_right, 1)
    got_right = shifted(send_left, -1)
    own = call(
        own_columns_kernel,
        (meta, xt, source_emb, target_emb, c_own, keep_own, u, weight, fits),
        row,
        [rows_shape, ya_shape, kept(1), pltpu.VMEM((blocks, 8, BLK), f32)] + block_scratch + [wide]
        + [pltpu.VMEM((blocks, 1, BLK), f32)] * 2,
        LIMITS[3],
        6,
        (2, 3),
    )
    got_left = got_left + no_left[:, 0:1]
    got_right = got_right + no_right[:, 0:1]
    top = jnp.maximum(jnp.maximum(own, got_left), got_right)
    total = jnp.exp(own - top) + jnp.exp(got_left - top) + jnp.exp(got_right - top)
    target_potential = 0.5 * (log_tgt + twice - (top + jnp.log(total)).reshape(width))
    return potential.reshape(width), target_potential


def solution(mesh):
    return jax.shard_map(
        on_device,
        mesh=mesh,
        in_specs=(P(None, AXES), P(None, AXES), P(AXES), P(AXES), P(AXES), P()),
        out_specs=(P(AXES), P(AXES)),
        check_vma=False,
    )
```

```python
import functools

import jax
import jax.numpy as jnp
from jax import lax
from jax.experimental import pallas as pl
from jax.experimental.pallas import tpu as pltpu
from jax.sharding import PartitionSpec as P

BLK = 1024
P_DEV = 18
W = 64
DEPTH = 80
MOST = 21
KEEP_OWN = 11
KEEP_NEAR = 5
KEEP_FAR = 4
FLOOR = -1.0e30
SPAN = 75.0
ROWS = 256
LIMITS = (8, 4, 18, 8)
AXES = ("grp", "dev")
f32 = jnp.float32
bf16 = jnp.bfloat16


def swapped(value, near):
    count = lax.axis_size(AXES)
    pairs = [(i, i + 1) for i in range(0 if near else 1, count - 1, 2)]
    return lax.ppermute(value, AXES, pairs + [(j, i) for i, j in pairs])


def near_side(meta):
    return 1 - 2 * (meta[0] & 1)


def place(meta, p):
    device = meta[0]
    blocks = meta[1]
    source = meta[3 + p] - device * blocks
    target = meta[3 + MOST + p] - device * blocks
    valid = (source >= 0) & (source < blocks)
    side = jnp.where(target < 0, -1, jnp.where(target >= blocks, 1, 0))
    return valid, jnp.clip(source, 0, blocks - 1), side, target - side * blocks


def list_rows(meta, side_wanted, rows):
    def step(p, count):
        valid, _, side, _ = place(meta, p)
        take = valid & (side == side_wanted)

        @pl.when(take)
        def _():
            rows[count] = p

        return count + take.astype(jnp.int32)

    return lax.fori_loop(0, MOST, step, jnp.int32(0))


def cells(block):
    return pl.ds(pl.multiple_of(block * BLK, BLK), BLK)


def two_at_a_time(start, stop, body):
    half = lax.shift_right_logical(stop - start, jnp.int32(1))

    @pl.loop(0, half)
    def _(n):
        body(start + 2 * n)
        body(start + 2 * n + 1)

    @pl.when(start + 2 * half < stop)
    def _():
        body(stop - 1)


def fill_offsets(y, c):
    width = c.shape[1]
    pots = y[:, width : width + 128].astype(f32)
    for t in range(width // BLK):
        rows = range(t * (BLK // 128), (t + 1) * (BLK // 128))
        row = jnp.concatenate([pots[r : r + 1, :] for r in rows], axis=1)
        c[:, t * BLK : (t + 1) * BLK] = 2.0 * row - norms(y, t)


def fill_targets(y, c, ya):
    for t in range(ya.shape[0]):
        ya[t, 0:W, :] = y[:, t * BLK : (t + 1) * BLK]
    fill_rows(c, ya)


def refill_targets(y, c, ya):
    for t in range(ya.shape[0]):
        pltpu.sync_copy(y.at[:, pl.ds(t * BLK, BLK)], ya.at[t, pl.ds(0, W), :])
    fill_rows(c, ya)


def fill_rows(c, ya):
    for t in range(ya.shape[0]):
        row = c[:, t * BLK : (t + 1) * BLK]
        high = row.astype(bf16).astype(f32)
        rest = row - high
        middle = rest.astype(bf16).astype(f32)
        low = rest - middle
        index = lax.broadcasted_iota(jnp.int32, (DEPTH - W, BLK), 0)
        extra = jnp.where(
            index == 0, high, jnp.where(index == 1, middle, jnp.where(index == 2, low, 0.0))
        )
        ya[t, W:DEPTH, :] = extra.astype(bf16)


def kernel_values(xt, ya, s, t, sums, keep, slot):
    for first in range(0, BLK, ROWS):
        here = pl.ds(first, ROWS)
        k = jnp.exp(jnp.dot(xt[s, here, :], ya[t], preferred_element_type=f32))
        if sums is not None:
            part = k[:, 0:128]
            for j in range(128, BLK, 128):
                part = part + k[:, j : j + 128]
            sums[s, here, :] += part
        if keep is not None:
            keep[slot, here, :] = k.astype(bf16)


def row_pairs(meta, rows, count, xt, ya, sums, keep, capacity):
    def kept(n):
        _, s, _, t = place(meta, rows[n])
        kernel_values(xt, ya, s, t, sums, keep, n)

    two_at_a_time(0, jnp.minimum(count, capacity), kept)

    @pl.loop(jnp.minimum(count, capacity), count)
    def _(n):
        _, s, _, t = place(meta, rows[n])
        kernel_values(xt, ya, s, t, sums, None, 0)


def column_pairs(meta, rows, count, xt, ya, u, keep, capacity, spare, spare_slot, totals, base):
    def add(s, t, k):
        totals[base + t] += jnp.dot(u[s].astype(bf16), k, preferred_element_type=f32)

    def kept(n):
        _, s, _, t = place(meta, rows[n])
        add(s, t, keep[n])

    two_at_a_time(0, jnp.minimum(count, capacity), kept)

    @pl.loop(jnp.minimum(count, capacity), count)
    def _(n):
        _, s, _, t = place(meta, rows[n])
        kernel_values(xt, ya, s, t, None, spare, spare_slot)
        add(s, t, spare[spare_slot])


def lane_sums(part):
    return jnp.sum(jnp.transpose(part), axis=0, keepdims=True)


def norms(x, s):
    full = x[:, s * BLK : (s + 1) * BLK].astype(f32)
    return jnp.sum(full * full, axis=0, keepdims=True)


def logs(total):
    return jnp.where(total > 0.0, jnp.log(jnp.where(total > 0.0, total, 1.0)), FLOOR)


STEP = 128


def fetch(meta, p, x, ys, cs, x_block, y_block, c_block):
    _, s, side, t = place(meta, p)
    pltpu.sync_copy(x.at[:, cells(s)], x_block)
    near = near_side(meta)
    for side_here, y, c in zip((near, 0, -near), ys, cs):
        if y is None:
            continue

        @pl.when(side == side_here)
        def _():
            pltpu.sync_copy(y.at[:, cells(t)], y_block)
            c_block[...] = c[:, cells(t)]


def products(x_block, first, y_block):
    x_part = x_block[:, pl.ds(pl.multiple_of(first, STEP), STEP)]
    return 2.0 * lax.dot_general(
        x_part, y_block[...], (((0,), (0,)), ((), ())), preferred_element_type=f32
    )


def general_rows(meta, x, ys, cs, x_block, y_block, c_block, top, mass, log_rows):
    @pl.loop(0, MOST)
    def _(p):
        valid, s, _, _ = place(meta, p)
        before_valid, before, _, _ = place(meta, jnp.maximum(p - 1, 0))

        @pl.when(valid)
        def _():
            @pl.when((p == 0) | jnp.logical_not(before_valid) | (before != s))
            def _():
                top[...] = jnp.full_like(top, FLOOR)
                mass[...] = jnp.zeros_like(mass)

            fetch(meta, p, x, ys, cs, x_block, y_block, c_block)

            @pl.loop(0, BLK // STEP)
            def _(q):
                here = pl.ds(pl.multiple_of(q * STEP, STEP), STEP)
                logits = products(x_block, q * STEP, y_block) + c_block[...]
                old = top[here, :]
                new = jnp.maximum(old, jnp.max(logits, axis=1, keepdims=True))
                terms = jnp.sum(jnp.exp(logits - new[:, 0:1]), axis=1, keepdims=True)
                mass[here, :] = mass[here, :] * jnp.exp(old - new) + terms
                top[here, :] = new

            log_rows[:, cells(s)] = jnp.transpose(top[...] + jnp.log(mass[...]))[0:1, :]


def general_columns(
    meta, own, base, x, ys, cs, x_block, y_block, c_block, weight, column, col_top, col_mass
):
    @pl.loop(0, MOST)
    def _(p):
        valid, s, side, t = place(meta, p)
        wanted = (side == 0) == own

        @pl.when(valid & wanted)
        def _():
            fetch(meta, p, x, ys, cs, x_block, y_block, c_block)
            column[...] = jnp.transpose(jnp.broadcast_to(weight[:, cells(s)], (128, BLK)))
            slot = base(side, t)

            @pl.loop(0, BLK // STEP)
            def _(q):
                here = pl.ds(pl.multiple_of(q * STEP, STEP), STEP)
                logits = products(x_block, q * STEP, y_block) + c_block[...] + column[here, 0:1]
                old = col_top[slot]
                new = jnp.maximum(old, jnp.max(logits, axis=0, keepdims=True))
                terms = jnp.sum(jnp.exp(logits - new[0:1, :]), axis=0, keepdims=True)
                col_mass[slot] = col_mass[slot] * jnp.exp(old - new) + terms
                col_top[slot] = new


def own_rows_kernel(meta, x, y, xt, keep, total, c, norm, rows, ya, sums):
    blocks = sums.shape[0]
    for s in range(blocks):
        norm[:, s * BLK : (s + 1) * BLK] = norms(x, s)
        doubled = 2.0 * x[:, s * BLK : (s + 1) * BLK].astype(f32)
        xt[s, :, 0:W] = jnp.transpose(doubled).astype(bf16)
        xt[s, :, W:DEPTH] = jnp.ones((BLK, DEPTH - W), bf16)
    fill_offsets(y, c)
    fill_targets(y, c, ya)
    sums[...] = jnp.zeros_like(sums)
    count = list_rows(meta, 0, rows)
    row_pairs(meta, rows, count, xt, ya, sums, keep, KEEP_OWN)
    for s in range(blocks):
        total[:, s * BLK : (s + 1) * BLK] = lane_sums(sums[s])


def near_rows_kernel(meta, xt, y, keep, sums, c, rows, ya):
    fill_offsets(y, c)
    fill_targets(y, c, ya)
    sums[...] = jnp.zeros_like(sums)
    count = list_rows(meta, near_side(meta), rows)
    row_pairs(meta, rows, count, xt, ya, sums, keep, KEEP_NEAR)


def settle_kernel(
    meta, xt, x, y_near, c_near, y_own, c_own, y_far, norm, own_total, near_sums, keep_near, log_src,
    potential, send_near, send_far, u, weight, fits, no_far,
    rows_near, rows_far, c_far, ya, keep, sums, totals,
    x_block, y_block, c_block, col_top, col_mass,
):
    blocks = u.shape[0]
    top, mass, column = sums.at[0], sums.at[1], sums.at[2]
    fill_offsets(y_far, c_far)
    fill_targets(y_far, c_far, ya)
    sums[...] = jnp.zeros_like(sums)
    near = near_side(meta)
    count_near = list_rows(meta, near, rows_near)
    count_far = list_rows(meta, -near, rows_far)
    row_pairs(meta, rows_far, count_far, xt, ya, sums, keep, KEEP_FAR)

    lowest = jnp.minimum(jnp.minimum(c_near[...], c_far[...]), c_own[...])
    x2 = jnp.max(norm[...], axis=1, keepdims=True)
    c_min = jnp.min(lowest, axis=1, keepdims=True)
    y2 = jnp.maximum(10.0 - c_min, 0.0)
    extent = x2 + 10.0 + 2.0 * jnp.sqrt(x2) * jnp.sqrt(y2) - c_min
    in_range = jnp.max(extent) <= SPAN
    alone = (meta[0] == 0) | (meta[0] == meta[2] - 1)
    no_far[...] = jnp.full_like(no_far, jnp.where(alone, FLOOR, 0.0))
    fits[...] = jnp.broadcast_to(jnp.where(extent <= SPAN, 1.0, 0.0), fits.shape)
    offset = lambda side, t: jnp.where(side == near, t, blocks + t)

    @pl.when(in_range)
    def _():
        index = lax.broadcasted_iota(jnp.int32, (8, BLK), 0)
        for s in range(blocks):
            here = slice(s * BLK, (s + 1) * BLK)
            total = own_total[:, here] + lane_sums(near_sums[s] + sums[s])
            w = log_src[:, here] - jnp.log(total)
            weight[:, here] = w
            value = jnp.exp(w)
            high = value.astype(bf16).astype(f32)
            u[s] = jnp.where(index == 0, high, jnp.where(index == 1, value - high, 0.0))
        totals[...] = jnp.zeros_like(totals)
        column_pairs(
            meta, rows_far, count_far, xt, ya, u, keep, KEEP_FAR,
            keep, KEEP_FAR, totals, blocks,
        )

        @pl.when(count_near > KEEP_NEAR)
        def _():
            refill_targets(y_near, c_near, ya)

        column_pairs(
            meta, rows_near, count_near, xt, ya, u, keep_near, KEEP_NEAR,
            keep, KEEP_FAR, totals, 0,
        )
        for t in range(blocks):
            here = slice(t * BLK, (t + 1) * BLK)
            send_near[:, here] = logs(jnp.sum(totals[t], axis=0, keepdims=True))
            send_far[:, here] = logs(jnp.sum(totals[blocks + t], axis=0, keepdims=True))

    @pl.when(jnp.logical_not(in_range))
    def _():
        ys = (y_near, y_own, y_far)
        cs = (c_near, c_own, c_far)
        general_rows(meta, x, ys, cs, x_block, y_block, c_block, top, mass, weight)
        weight[...] = log_src[...] - weight[...]
        u[...] = jnp.zeros_like(u)
        col_top[...] = jnp.full_like(col_top, FLOOR)
        col_mass[...] = jnp.zeros_like(col_mass)
        general_columns(
            meta, False, offset, x, ys, cs, x_block, y_block, c_block, weight, column,
            col_top, col_mass,
        )
        for t in range(blocks):
            here = slice(t * BLK, (t + 1) * BLK)
            send_near[:, here] = (col_top[t] + logs(col_mass[t]))[0:1, :]
            send_far[:, here] = (col_top[blocks + t] + logs(col_mass[blocks + t]))[0:1, :]

    potential[...] = 0.5 * (weight[...] + norm[...])


def own_columns_kernel(
    meta, xt, x, y, c, keep, u, weight, fits,
    out,
    rows, ya, spare, totals, x_block, y_block, c_block, column, col_top, col_mass,
):
    blocks = u.shape[0]
    in_range = jnp.max(fits[...]) > 0.5
    count = list_rows(meta, 0, rows)

    @pl.when(in_range)
    def _():
        @pl.when(count > KEEP_OWN)
        def _():
            refill_targets(y, c, ya)

        totals[...] = jnp.zeros_like(totals)
        column_pairs(meta, rows, count, xt, ya, u, keep, KEEP_OWN, spare, 0, totals, 0)
        for t in range(blocks):
            out[:, t * BLK : (t + 1) * BLK] = logs(jnp.sum(totals[t], axis=0, keepdims=True))

    @pl.when(jnp.logical_not(in_range))
    def _():
        col_top[...] = jnp.full_like(col_top, FLOOR)
        col_mass[...] = jnp.zeros_like(col_mass)
        general_columns(
            meta, True, lambda side, t: t, x, (None, y, None), (None, c, None),
            x_block, y_block, c_block, weight, column, col_top, col_mass,
        )
        for t in range(blocks):
            here = slice(t * BLK, (t + 1) * BLK)
            out[:, here] = (col_top[t] + logs(col_mass[t]))[0:1, :]


def call(kernel, operands, outs, scratch, limit, pairs, outside=()):
    in_vmem = pl.BlockSpec(memory_space=pltpu.VMEM)
    in_smem = pl.BlockSpec(memory_space=pltpu.SMEM)
    anywhere = pl.BlockSpec(memory_space=pl.ANY)
    return pl.pallas_call(
        kernel,
        out_shape=outs,
        in_specs=[in_smem]
        + [anywhere if n in outside else in_vmem for n in range(1, len(operands))],
        out_specs=jax.tree.map(lambda _: in_vmem, outs),
        scratch_shapes=scratch,
        compiler_params=pltpu.CompilerParams(vmem_limit_bytes=limit << 20),
        cost_estimate=pl.CostEstimate(
            flops=pairs * 2 * BLK * BLK * 256, bytes_accessed=1 << 20, transcendentals=pairs * BLK * BLK
        ),
    )(*operands)


def on_device(source_emb, target_emb, target_pot, log_src, log_tgt, pair_list):
    position = lax.axis_index(AXES)
    width = source_emb.shape[1]
    blocks = width // BLK
    row = jax.ShapeDtypeStruct((1, width), f32)
    pots = target_pot.reshape(width // 128, 128)
    pots = jnp.pad(pots, ((0, W - width // 128), (0, 0)))
    packed = jnp.concatenate([target_emb, pots], axis=1)
    from_near = swapped(packed, True)
    from_far = swapped(packed, False)
    twice = 2.0 * target_pot.astype(f32)

    mine = lax.dynamic_slice_in_dim(pair_list, position * P_DEV, MOST, 0)
    meta = jnp.concatenate(
        [jnp.stack([position, jnp.int32(blocks), jnp.int32(lax.axis_size(AXES))]).astype(jnp.int32), mine[:, 0], mine[:, 1]]
    )

    def kept(n):
        return pltpu.VMEM((n, BLK, BLK), bf16)

    sums_shape = (blocks, BLK, 128)
    ya_shape = pltpu.VMEM((blocks, DEPTH, BLK), bf16)
    rows_shape = pltpu.SMEM((MOST,), jnp.int32)
    row_here = pltpu.VMEM((1, width), f32)
    xt, keep_own, own_total, c_own, norm = call(
        own_rows_kernel,
        (meta, source_emb, packed),
        (pltpu.VMEM((blocks, BLK, DEPTH), bf16), kept(KEEP_OWN), row_here, row_here, row_here),
        [rows_shape, ya_shape, pltpu.VMEM(sums_shape, f32)],
        LIMITS[0],
        9,
    )
    keep_near, near_sums, c_near = call(
        near_rows_kernel,
        (meta, xt, from_near),
        (kept(KEEP_NEAR), pltpu.VMEM(sums_shape, f32), row_here),
        [rows_shape, ya_shape],
        LIMITS[1],
        4,
    )
    block_scratch = [pltpu.VMEM((W, BLK), bf16)] * 2 + [pltpu.VMEM((1, BLK), f32)]
    wide = pltpu.VMEM((BLK, 128), f32)
    one = jax.ShapeDtypeStruct((1, 128), f32)
    potential, send_near, send_far, u, weight, fits, no_far = call(
        settle_kernel,
        (meta, xt, source_emb, from_near, c_near, target_emb, c_own, from_far, norm,
         own_total, near_sums, keep_near, log_src.reshape(1, width)),
        (row, row, row, pltpu.VMEM((blocks, 8, BLK), f32), row, one, one),
        [rows_shape, rows_shape, row_here, ya_shape, kept(KEEP_FAR + 1),
         pltpu.VMEM(sums_shape, f32), pltpu.VMEM((2 * blocks, 8, BLK), f32)] + block_scratch
        + [pltpu.VMEM((2 * blocks, 1, BLK), f32)] * 2,
        LIMITS[2],
        8,
        (2, 3, 5),
    )
    got_far = swapped(send_far, False)
    got_near = swapped(send_near, True)
    own = call(
        own_columns_kernel,
        (meta, xt, source_emb, target_emb, c_own, keep_own, u, weight, fits),
        row,
        [rows_shape, ya_shape, kept(1), pltpu.VMEM((blocks, 8, BLK), f32)] + block_scratch + [wide]
        + [pltpu.VMEM((blocks, 1, BLK), f32)] * 2,
        LIMITS[3],
        6,
        (2, 3),
    )
    got_far = got_far + no_far[:, 0:1]
    top = jnp.maximum(jnp.maximum(got_far, got_near), own)
    total = jnp.exp(got_far - top) + jnp.exp(got_near - top) + jnp.exp(own - top)
    target_potential = 0.5 * (log_tgt + twice - (top + jnp.log(total)).reshape(width))
    return potential.reshape(width), target_potential


def solution(mesh):
    return jax.shard_map(
        on_device,
        mesh=mesh,
        in_specs=(P(None, AXES), P(None, AXES), P(AXES), P(AXES), P(AXES), P()),
        out_specs=(P(AXES), P(AXES)),
        check_vma=False,
    )
```

```python
import functools

import jax
import jax.numpy as jnp
from jax import lax
from jax.experimental import pallas as pl
from jax.experimental.pallas import tpu as pltpu
from jax.sharding import PartitionSpec as P

BLK = 1024
P_DEV = 18
W = 64
DEPTH = 80
MOST = 21
KEEP_OWN = 7
KEEP_NEAR = 7
KEEP_FAR = 6
SLOTS = 4
FLOOR = -1.0e30
SPAN = 75.0
ROWS = 256
LIMITS = (10, 4, 21, 12)
AXES = ("grp", "dev")
f32 = jnp.float32
bf16 = jnp.bfloat16


def swapped(value, near):
    count = lax.axis_size(AXES)
    pairs = [(i, i + 1) for i in range(0 if near else 1, count - 1, 2)]
    return lax.ppermute(value, AXES, pairs + [(j, i) for i, j in pairs])


def near_side(meta):
    return 1 - 2 * (meta[0] & 1)


def place(meta, p):
    device = meta[0]
    blocks = meta[1]
    source = meta[3 + p] - device * blocks
    target = meta[3 + MOST + p] - device * blocks
    valid = (source >= 0) & (source < blocks)
    side = jnp.where(target < 0, -1, jnp.where(target >= blocks, 1, 0))
    return valid, jnp.clip(source, 0, blocks - 1), side, target - side * blocks


def list_rows(meta, *wanted):
    counts = [jnp.int32(0)] * len(wanted)
    for p in range(MOST):
        valid, _, side, _ = place(meta, p)
        for n, (side_wanted, rows) in enumerate(wanted):
            rows[counts[n]] = p
            counts[n] = counts[n] + (valid & (side == side_wanted)).astype(jnp.int32)
    return counts


def cells(block):
    return pl.ds(pl.multiple_of(block * BLK, BLK), BLK)


def two_at_a_time(start, stop, body):
    half = lax.shift_right_logical(stop - start, jnp.int32(1))

    @pl.loop(0, half)
    def _(n):
        body(start + 2 * n)
        body(start + 2 * n + 1)

    @pl.when(start + 2 * half < stop)
    def _():
        body(stop - 1)


def fill_offsets(y, c):
    width = c.shape[1]
    pots = y[:, width : width + 128].astype(f32)
    for t in range(width // BLK):
        rows = range(t * (BLK // 128), (t + 1) * (BLK // 128))
        row = jnp.concatenate([pots[r : r + 1, :] for r in rows], axis=1)
        c[:, t * BLK : (t + 1) * BLK] = 2.0 * row - norms(y, t)


def fill_targets(y, c, ya):
    for t in range(ya.shape[0]):
        ya[t, 0:W, :] = y[:, t * BLK : (t + 1) * BLK]
    fill_rows(c, ya)


def refill_targets(y, c, ya):
    for t in range(ya.shape[0]):
        pltpu.sync_copy(y.at[:, pl.ds(t * BLK, BLK)], ya.at[t, pl.ds(0, W), :])
    fill_rows(c, ya)


def fill_rows(c, ya):
    for t in range(ya.shape[0]):
        row = c[:, t * BLK : (t + 1) * BLK]
        high = row.astype(bf16).astype(f32)
        rest = row - high
        middle = rest.astype(bf16).astype(f32)
        low = rest - middle
        index = lax.broadcasted_iota(jnp.int32, (DEPTH - W, BLK), 0)
        extra = jnp.where(
            index == 0, high, jnp.where(index == 1, middle, jnp.where(index == 2, low, 0.0))
        )
        ya[t, W:DEPTH, :] = extra.astype(bf16)


def kernel_values(xt, ya, s, t, sums, keep, slot):
    for first in range(0, BLK, ROWS):
        here = pl.ds(first, ROWS)
        k = jnp.exp(jnp.dot(xt[s, here, :], ya[t], preferred_element_type=f32))
        if sums is not None:
            part = k[:, 0:128]
            for j in range(128, BLK, 128):
                part = part + k[:, j : j + 128]
            sums[s, here, :] += part
        if keep is not None:
            keep[slot, here, :] = k.astype(bf16)


def row_pairs(meta, rows, count, xt, ya, sums, keep, capacity):
    def kept(n):
        _, s, _, t = place(meta, rows[n])
        kernel_values(xt, ya, s, t, sums, keep, n)

    two_at_a_time(0, jnp.minimum(count, capacity), kept)

    @pl.loop(jnp.minimum(count, capacity), count)
    def _(n):
        _, s, _, t = place(meta, rows[n])
        kernel_values(xt, ya, s, t, sums, None, 0)


def column_pairs(meta, rows, count, xt, ya, u, keep, capacity, spare, spare_slot, totals, base):
    def add(s, t, k):
        totals[base + t] += jnp.dot(u[s].astype(bf16), k, preferred_element_type=f32)

    def kept(n):
        _, s, _, t = place(meta, rows[n])
        add(s, t, keep[n])

    two_at_a_time(0, jnp.minimum(count, capacity), kept)

    if spare is None:
        return

    @pl.loop(jnp.minimum(count, capacity), count)
    def _(n):
        _, s, _, t = place(meta, rows[n])
        kernel_values(xt, ya, s, t, None, spare, spare_slot)
        add(s, t, spare[spare_slot])


def lane_sums(part):
    return jnp.sum(jnp.transpose(part), axis=0, keepdims=True)


def norms(x, s):
    full = x[:, s * BLK : (s + 1) * BLK].astype(f32)
    return jnp.sum(full * full, axis=0, keepdims=True)


def logs(total):
    return jnp.where(total > 0.0, jnp.log(jnp.where(total > 0.0, total, 1.0)), FLOOR)


STEP = 128


def fetch(meta, p, x, ys, cs, x_block, y_block, c_block):
    _, s, side, t = place(meta, p)
    pltpu.sync_copy(x.at[:, cells(s)], x_block)
    near = near_side(meta)
    for side_here, y, c in zip((near, 0, -near), ys, cs):
        if y is None:
            continue

        @pl.when(side == side_here)
        def _():
            pltpu.sync_copy(y.at[:, cells(t)], y_block)
            c_block[...] = c[:, cells(t)]


def products(x_block, first, y_block):
    x_part = x_block[:, pl.ds(pl.multiple_of(first, STEP), STEP)]
    return 2.0 * lax.dot_general(
        x_part, y_block[...], (((0,), (0,)), ((), ())), preferred_element_type=f32
    )


def general_rows(meta, x, ys, cs, x_block, y_block, c_block, top, mass, log_rows):
    @pl.loop(0, MOST)
    def _(p):
        valid, s, _, _ = place(meta, p)
        before_valid, before, _, _ = place(meta, jnp.maximum(p - 1, 0))

        @pl.when(valid)
        def _():
            @pl.when((p == 0) | jnp.logical_not(before_valid) | (before != s))
            def _():
                top[...] = jnp.full_like(top, FLOOR)
                mass[...] = jnp.zeros_like(mass)

            fetch(meta, p, x, ys, cs, x_block, y_block, c_block)

            @pl.loop(0, BLK // STEP)
            def _(q):
                here = pl.ds(pl.multiple_of(q * STEP, STEP), STEP)
                logits = products(x_block, q * STEP, y_block) + c_block[...]
                old = top[here, :]
                new = jnp.maximum(old, jnp.max(logits, axis=1, keepdims=True))
                terms = jnp.sum(jnp.exp(logits - new[:, 0:1]), axis=1, keepdims=True)
                mass[here, :] = mass[here, :] * jnp.exp(old - new) + terms
                top[here, :] = new

            log_rows[:, cells(s)] = jnp.transpose(top[...] + jnp.log(mass[...]))[0:1, :]


def general_columns(
    meta, own, base, x, ys, cs, x_block, y_block, c_block, weight, column, col_top, col_mass
):
    @pl.loop(0, MOST)
    def _(p):
        valid, s, side, t = place(meta, p)
        wanted = (side == 0) == own

        @pl.when(valid & wanted)
        def _():
            fetch(meta, p, x, ys, cs, x_block, y_block, c_block)
            column[...] = jnp.transpose(jnp.broadcast_to(weight[:, cells(s)], (128, BLK)))
            slot = base(side, t)

            @pl.loop(0, BLK // STEP)
            def _(q):
                here = pl.ds(pl.multiple_of(q * STEP, STEP), STEP)
                logits = products(x_block, q * STEP, y_block) + c_block[...] + column[here, 0:1]
                old = col_top[slot]
                new = jnp.maximum(old, jnp.max(logits, axis=0, keepdims=True))
                terms = jnp.sum(jnp.exp(logits - new[0:1, :]), axis=0, keepdims=True)
                col_mass[slot] = col_mass[slot] * jnp.exp(old - new) + terms
                col_top[slot] = new


def spill_out(spill, slots, sems, n):
    here = lax.rem(n, slots.shape[0])
    return pltpu.make_async_copy(slots.at[here], spill.at[n], sems.at[here])


def spill_in(spill, slots, sems, n):
    here = lax.rem(n, slots.shape[0])
    return pltpu.make_async_copy(spill.at[n], slots.at[here], sems.at[here])


def own_rows_kernel(
    meta, x, y, xt, keep, spill, total, c, norm, rows, ya, sums, slots, sems
):
    blocks = sums.shape[0]
    for s in range(blocks):
        norm[:, s * BLK : (s + 1) * BLK] = norms(x, s)
        doubled = 2.0 * x[:, s * BLK : (s + 1) * BLK].astype(f32)
        xt[s, :, 0:W] = jnp.transpose(doubled).astype(bf16)
        xt[s, :, W:DEPTH] = jnp.ones((BLK, DEPTH - W), bf16)
    fill_offsets(y, c)
    fill_targets(y, c, ya)
    sums[...] = jnp.zeros_like(sums)
    (count,) = list_rows(meta, (0, rows))
    kept = jnp.minimum(count, KEEP_OWN)
    row_pairs(meta, rows, kept, xt, ya, sums, keep, KEEP_OWN)
    extra = count - kept

    @pl.loop(0, extra)
    def _(n):
        @pl.when(n >= slots.shape[0])
        def _():
            spill_out(spill, slots, sems, n - slots.shape[0]).wait()

        _, s, _, t = place(meta, rows[kept + n])
        kernel_values(xt, ya, s, t, sums, slots, lax.rem(n, slots.shape[0]))
        spill_out(spill, slots, sems, n).start()

    @pl.loop(jnp.maximum(extra - slots.shape[0], 0), extra)
    def _(n):
        spill_out(spill, slots, sems, n).wait()

    for s in range(blocks):
        total[:, s * BLK : (s + 1) * BLK] = lane_sums(sums[s])


def near_rows_kernel(meta, xt, y, keep, sums, c, rows, ya):
    fill_offsets(y, c)
    fill_targets(y, c, ya)
    sums[...] = jnp.zeros_like(sums)
    (count,) = list_rows(meta, (near_side(meta), rows))
    row_pairs(meta, rows, count, xt, ya, sums, keep, KEEP_NEAR)


def settle_kernel(
    meta, xt, x, y_near, c_near, y_own, c_own, y_far, norm, own_total, near_sums, keep_near, log_src,
    potential, send_near, send_far, u, weight, fits, no_far,
    rows_near, rows_far, potential_row, potential_sem, c_far, ya, keep, sums, totals,
    x_block, y_block, c_block, col_top, col_mass,
):
    blocks = u.shape[0]
    top, mass, column = sums.at[0], sums.at[1], sums.at[2]
    fill_offsets(y_far, c_far)
    fill_targets(y_far, c_far, ya)
    sums[...] = jnp.zeros_like(sums)
    near = near_side(meta)
    count_near, count_far = list_rows(meta, (near, rows_near), (-near, rows_far))
    row_pairs(meta, rows_far, count_far, xt, ya, sums, keep, KEEP_FAR)

    lowest = jnp.minimum(jnp.minimum(c_near[...], c_far[...]), c_own[...])
    x2 = jnp.max(norm[...], axis=1, keepdims=True)
    c_min = jnp.min(lowest, axis=1, keepdims=True)
    y2 = jnp.maximum(10.0 - c_min, 0.0)
    extent = x2 + 10.0 + 2.0 * jnp.sqrt(x2) * jnp.sqrt(y2) - c_min
    in_range = jnp.max(extent) <= SPAN
    alone = (meta[0] == 0) | (meta[0] == meta[2] - 1)
    no_far[...] = jnp.full_like(no_far, jnp.where(alone, FLOOR, 0.0))
    fits[...] = jnp.broadcast_to(jnp.where(extent <= SPAN, 1.0, 0.0), fits.shape)
    offset = lambda side, t: jnp.where(side == near, t, blocks + t)

    @pl.when(in_range)
    def _():
        index = lax.broadcasted_iota(jnp.int32, (8, BLK), 0)
        for s in range(blocks):
            here = slice(s * BLK, (s + 1) * BLK)
            total = own_total[:, here] + lane_sums(near_sums[s] + sums[s])
            w = log_src[:, here] - jnp.log(total)
            weight[:, here] = w
            value = jnp.exp(w)
            high = value.astype(bf16).astype(f32)
            u[s] = jnp.where(index == 0, high, jnp.where(index == 1, value - high, 0.0))
        potential_row[...] = 0.5 * (weight[...] + norm[...])
        hand_over = pltpu.make_async_copy(potential_row, potential, potential_sem)
        hand_over.start()
        totals[...] = jnp.zeros_like(totals)
        column_pairs(
            meta, rows_far, count_far, xt, ya, u, keep, KEEP_FAR,
            keep, KEEP_FAR, totals, blocks,
        )

        @pl.when(count_near > KEEP_NEAR)
        def _():
            refill_targets(y_near, c_near, ya)

        column_pairs(
            meta, rows_near, count_near, xt, ya, u, keep_near, KEEP_NEAR,
            keep, KEEP_FAR, totals, 0,
        )
        for t in range(blocks):
            here = slice(t * BLK, (t + 1) * BLK)
            send_near[:, here] = logs(jnp.sum(totals[t], axis=0, keepdims=True))
            send_far[:, here] = logs(jnp.sum(totals[blocks + t], axis=0, keepdims=True))
        hand_over.wait()

    @pl.when(jnp.logical_not(in_range))
    def _():
        ys = (y_near, y_own, y_far)
        cs = (c_near, c_own, c_far)
        general_rows(meta, x, ys, cs, x_block, y_block, c_block, top, mass, weight)
        weight[...] = log_src[...] - weight[...]
        u[...] = jnp.zeros_like(u)
        col_top[...] = jnp.full_like(col_top, FLOOR)
        col_mass[...] = jnp.zeros_like(col_mass)
        general_columns(
            meta, False, offset, x, ys, cs, x_block, y_block, c_block, weight, column,
            col_top, col_mass,
        )
        for t in range(blocks):
            here = slice(t * BLK, (t + 1) * BLK)
            send_near[:, here] = (col_top[t] + logs(col_mass[t]))[0:1, :]
            send_far[:, here] = (col_top[blocks + t] + logs(col_mass[blocks + t]))[0:1, :]
        potential_row[...] = 0.5 * (weight[...] + norm[...])
        pltpu.sync_copy(potential_row, potential)


def own_columns_kernel(
    meta, x, y, c, keep, spill, u, weight, fits,
    out,
    rows, slots, sems, totals, x_block, y_block, c_block, column, col_top, col_mass,
):
    blocks = u.shape[0]
    in_range = jnp.max(fits[...]) > 0.5
    (count,) = list_rows(meta, (0, rows))

    @pl.when(in_range)
    def _():
        kept = jnp.minimum(count, KEEP_OWN)
        extra = count - kept

        @pl.loop(0, jnp.minimum(extra, slots.shape[0]))
        def _(n):
            spill_in(spill, slots, sems, n).start()

        totals[...] = jnp.zeros_like(totals)
        column_pairs(meta, rows, kept, None, None, u, keep, KEEP_OWN, None, 0, totals, 0)

        @pl.loop(0, extra)
        def _(n):
            spill_in(spill, slots, sems, n).wait()
            _, s, _, t = place(meta, rows[kept + n])
            values = slots[lax.rem(n, slots.shape[0])]
            totals[t] += jnp.dot(u[s].astype(bf16), values, preferred_element_type=f32)

            @pl.when(n + slots.shape[0] < extra)
            def _():
                spill_in(spill, slots, sems, n + slots.shape[0]).start()

        for t in range(blocks):
            out[:, t * BLK : (t + 1) * BLK] = logs(jnp.sum(totals[t], axis=0, keepdims=True))

    @pl.when(jnp.logical_not(in_range))
    def _():
        col_top[...] = jnp.full_like(col_top, FLOOR)
        col_mass[...] = jnp.zeros_like(col_mass)
        general_columns(
            meta, True, lambda side, t: t, x, (None, y, None), (None, c, None),
            x_block, y_block, c_block, weight, column, col_top, col_mass,
        )
        for t in range(blocks):
            here = slice(t * BLK, (t + 1) * BLK)
            out[:, here] = (col_top[t] + logs(col_mass[t]))[0:1, :]


def call(kernel, operands, outs, scratch, limit, pairs, outside=(), outside_outs=()):
    in_vmem = pl.BlockSpec(memory_space=pltpu.VMEM)
    in_smem = pl.BlockSpec(memory_space=pltpu.SMEM)
    anywhere = pl.BlockSpec(memory_space=pl.ANY)
    return pl.pallas_call(
        kernel,
        out_shape=outs,
        in_specs=[in_smem]
        + [anywhere if n in outside else in_vmem for n in range(1, len(operands))],
        out_specs=tuple(
            anywhere if out in outside_outs else in_vmem for out in range(len(outs))
        ),
        scratch_shapes=scratch,
        compiler_params=pltpu.CompilerParams(vmem_limit_bytes=limit << 20),
        cost_estimate=pl.CostEstimate(
            flops=pairs * 2 * BLK * BLK * 256, bytes_accessed=1 << 20, transcendentals=pairs * BLK * BLK
        ),
    )(*operands)


def on_device(source_emb, target_emb, target_pot, log_src, log_tgt, pair_list):
    position = lax.axis_index(AXES)
    width = source_emb.shape[1]
    blocks = width // BLK
    row = jax.ShapeDtypeStruct((1, width), f32)
    pots = target_pot.reshape(width // 128, 128)
    pots = jnp.pad(pots, ((0, W - width // 128), (0, 0)))
    packed = jnp.concatenate([target_emb, pots], axis=1)
    from_near = swapped(packed, True)
    from_far = swapped(packed, False)
    twice = 2.0 * target_pot.astype(f32)

    mine = lax.dynamic_slice_in_dim(pair_list, position * P_DEV, MOST, 0)
    meta = jnp.concatenate(
        [jnp.stack([position, jnp.int32(blocks), jnp.int32(lax.axis_size(AXES))]).astype(jnp.int32), mine[:, 0], mine[:, 1]]
    )

    def kept(n):
        return pltpu.VMEM((n, BLK, BLK), bf16)

    sums_shape = (blocks, BLK, 128)
    ya_shape = pltpu.VMEM((blocks, DEPTH, BLK), bf16)
    rows_shape = pltpu.SMEM((MOST + 1,), jnp.int32)
    row_here = pltpu.VMEM((1, width), f32)
    xt, keep_own, spill, own_total, c_own, norm = call(
        own_rows_kernel,
        (meta, source_emb, packed),
        (pltpu.VMEM((blocks, BLK, DEPTH), bf16), kept(KEEP_OWN),
         jax.ShapeDtypeStruct((MOST - KEEP_OWN, BLK, BLK), bf16), row_here, row_here, row_here),
        [rows_shape, ya_shape, pltpu.VMEM(sums_shape, f32), kept(2), pltpu.SemaphoreType.DMA((2,))],
        LIMITS[0],
        9,
        (),
        (2,),
    )
    keep_near, near_sums, c_near = call(
        near_rows_kernel,
        (meta, xt, from_near),
        (kept(KEEP_NEAR), pltpu.VMEM(sums_shape, f32), row_here),
        [rows_shape, ya_shape],
        LIMITS[1],
        4,
    )
    block_scratch = [pltpu.VMEM((W, BLK), bf16)] * 2 + [pltpu.VMEM((1, BLK), f32)]
    wide = pltpu.VMEM((BLK, 128), f32)
    one = jax.ShapeDtypeStruct((1, 128), f32)
    potential, send_near, send_far, u, weight, fits, no_far = call(
        settle_kernel,
        (meta, xt, source_emb, from_near, c_near, target_emb, c_own, from_far, norm,
         own_total, near_sums, keep_near, log_src.reshape(1, width)),
        (row, row, row, pltpu.VMEM((blocks, 8, BLK), f32), row, one, one),
        [rows_shape, rows_shape, row_here, pltpu.SemaphoreType.DMA, row_here, ya_shape, kept(KEEP_FAR + 1),
         pltpu.VMEM(sums_shape, f32), pltpu.VMEM((2 * blocks, 8, BLK), f32)] + block_scratch
        + [pltpu.VMEM((2 * blocks, 1, BLK), f32)] * 2,
        LIMITS[2],
        8,
        (2, 3, 5),
        (0,),
    )
    got_far = swapped(send_far, False)
    got_near = swapped(send_near, True)
    (own,) = call(
        own_columns_kernel,
        (meta, source_emb, target_emb, c_own, keep_own, spill, u, weight, fits),
        (row,),
        [rows_shape, kept(SLOTS), pltpu.SemaphoreType.DMA((SLOTS,)), pltpu.VMEM((blocks, 8, BLK), f32)] + block_scratch + [wide]
        + [pltpu.VMEM((blocks, 1, BLK), f32)] * 2,
        LIMITS[3],
        6,
        (1, 2, 5),
    )
    got_far = got_far + no_far[:, 0:1]
    top = jnp.maximum(jnp.maximum(got_far, got_near), own)
    total = jnp.exp(got_far - top) + jnp.exp(got_near - top) + jnp.exp(own - top)
    target_potential = 0.5 * (log_tgt + twice - (top + jnp.log(total)).reshape(width))
    return potential.reshape(width), target_potential


def solution(mesh):
    return jax.shard_map(
        on_device,
        mesh=mesh,
        in_specs=(P(None, AXES), P(None, AXES), P(AXES), P(AXES), P(AXES), P()),
        out_specs=(P(AXES), P(AXES)),
        check_vma=False,
    )
```

```python
import functools

import jax
import jax.numpy as jnp
from jax import lax
from jax.experimental import pallas as pl
from jax.experimental.pallas import tpu as pltpu
from jax.sharding import PartitionSpec as P

BLK = 1024
P_DEV = 18
W = 64
DEPTH = 80
MOST = 21
KEEP_OWN = 7
KEEP_NEAR = 7
KEEP_FAR = 8
SLOTS = 4
FLOOR = -1.0e30
SPAN = 75.0
ROWS = 256
LIMITS = (10, 6, 25, 12)
AXES = ("grp", "dev")
f32 = jnp.float32
bf16 = jnp.bfloat16


def swapped(value, near):
    count = lax.axis_size(AXES)
    pairs = [(i, i + 1) for i in range(0 if near else 1, count - 1, 2)]
    return lax.ppermute(value, AXES, pairs + [(j, i) for i, j in pairs])


def near_side(meta):
    return 1 - 2 * (meta[0] & 1)


def place(meta, p):
    device = meta[0]
    blocks = meta[1]
    source = meta[3 + p] - device * blocks
    target = meta[3 + MOST + p] - device * blocks
    valid = (source >= 0) & (source < blocks)
    side = jnp.where(target < 0, -1, jnp.where(target >= blocks, 1, 0))
    return valid, jnp.clip(source, 0, blocks - 1), side, target - side * blocks


def list_rows(meta, *wanted):
    counts = [jnp.int32(0)] * len(wanted)
    for p in range(MOST):
        valid, _, side, _ = place(meta, p)
        for n, (side_wanted, rows) in enumerate(wanted):
            rows[counts[n]] = p
            counts[n] = counts[n] + (valid & (side == side_wanted)).astype(jnp.int32)
    return counts


def cells(block):
    return pl.ds(pl.multiple_of(block * BLK, BLK), BLK)


def two_at_a_time(start, stop, body):
    half = lax.shift_right_logical(stop - start, jnp.int32(1))

    @pl.loop(0, half)
    def _(n):
        body(start + 2 * n)
        body(start + 2 * n + 1)

    @pl.when(start + 2 * half < stop)
    def _():
        body(stop - 1)


def fill_offsets(y, c):
    width = c.shape[1]
    pots = y[:, width : width + 128].astype(f32)
    for t in range(width // BLK):
        rows = range(t * (BLK // 128), (t + 1) * (BLK // 128))
        row = jnp.concatenate([pots[r : r + 1, :] for r in rows], axis=1)
        c[:, t * BLK : (t + 1) * BLK] = 2.0 * row - norms(y, t)


def fill_targets(y, c, ya):
    for t in range(ya.shape[0]):
        ya[t, 0:W, :] = y[:, t * BLK : (t + 1) * BLK]
    fill_rows(c, ya)


def refill_targets(y, c, ya):
    for t in range(ya.shape[0]):
        pltpu.sync_copy(y.at[:, pl.ds(t * BLK, BLK)], ya.at[t, pl.ds(0, W), :])
    fill_rows(c, ya)


def fill_rows(c, ya):
    for t in range(ya.shape[0]):
        row = c[:, t * BLK : (t + 1) * BLK]
        high = row.astype(bf16).astype(f32)
        rest = row - high
        middle = rest.astype(bf16).astype(f32)
        low = rest - middle
        index = lax.broadcasted_iota(jnp.int32, (DEPTH - W, BLK), 0)
        extra = jnp.where(
            index == 0, high, jnp.where(index == 1, middle, jnp.where(index == 2, low, 0.0))
        )
        ya[t, W:DEPTH, :] = extra.astype(bf16)


def kernel_values(xt, ya, s, t, sums, keep, slot):
    for first in range(0, BLK, ROWS):
        here = pl.ds(first, ROWS)
        k = jnp.exp(jnp.dot(xt[s, here, :], ya[t], preferred_element_type=f32))
        if sums is not None:
            part = k[:, 0:128]
            for j in range(128, BLK, 128):
                part = part + k[:, j : j + 128]
            sums[s, here, :] += part
        if keep is not None:
            keep[slot, here, :] = k.astype(bf16)


def row_pairs(meta, rows, count, xt, ya, sums, keep, capacity):
    def kept(n):
        _, s, _, t = place(meta, rows[n])
        kernel_values(xt, ya, s, t, sums, keep, n)

    two_at_a_time(0, jnp.minimum(count, capacity), kept)

    @pl.loop(jnp.minimum(count, capacity), count)
    def _(n):
        _, s, _, t = place(meta, rows[n])
        kernel_values(xt, ya, s, t, sums, None, 0)


def column_pairs(meta, rows, count, xt, ya, u, keep, capacity, spare, spare_slot, totals, base):
    def add(s, t, k):
        totals[base + t] += jnp.dot(u[s].astype(bf16), k, preferred_element_type=f32)

    def kept(n):
        _, s, _, t = place(meta, rows[n])
        add(s, t, keep[n])

    two_at_a_time(0, jnp.minimum(count, capacity), kept)

    if spare is None:
        return

    @pl.loop(jnp.minimum(count, capacity), count)
    def _(n):
        _, s, _, t = place(meta, rows[n])
        kernel_values(xt, ya, s, t, None, spare, spare_slot)
        add(s, t, spare[spare_slot])


def lane_sums(part):
    return jnp.sum(jnp.transpose(part), axis=0, keepdims=True)


def norms(x, s):
    full = x[:, s * BLK : (s + 1) * BLK].astype(f32)
    return jnp.sum(full * full, axis=0, keepdims=True)


def logs(total):
    return jnp.where(total > 0.0, jnp.log(jnp.where(total > 0.0, total, 1.0)), FLOOR)


STEP = 128


def fetch(meta, p, x, ys, cs, x_block, y_block, c_block):
    _, s, side, t = place(meta, p)
    pltpu.sync_copy(x.at[:, cells(s)], x_block)
    near = near_side(meta)
    for side_here, y, c in zip((near, 0, -near), ys, cs):
        if y is None:
            continue

        @pl.when(side == side_here)
        def _():
            pltpu.sync_copy(y.at[:, cells(t)], y_block)
            c_block[...] = c[:, cells(t)]


def products(x_block, first, y_block):
    x_part = x_block[:, pl.ds(pl.multiple_of(first, STEP), STEP)]
    return 2.0 * lax.dot_general(
        x_part, y_block[...], (((0,), (0,)), ((), ())), preferred_element_type=f32
    )


def general_rows(meta, x, ys, cs, x_block, y_block, c_block, top, mass, log_rows):
    @pl.loop(0, MOST)
    def _(p):
        valid, s, _, _ = place(meta, p)
        before_valid, before, _, _ = place(meta, jnp.maximum(p - 1, 0))

        @pl.when(valid)
        def _():
            @pl.when((p == 0) | jnp.logical_not(before_valid) | (before != s))
            def _():
                top[...] = jnp.full_like(top, FLOOR)
                mass[...] = jnp.zeros_like(mass)

            fetch(meta, p, x, ys, cs, x_block, y_block, c_block)

            @pl.loop(0, BLK // STEP)
            def _(q):
                here = pl.ds(pl.multiple_of(q * STEP, STEP), STEP)
                logits = products(x_block, q * STEP, y_block) + c_block[...]
                old = top[here, :]
                new = jnp.maximum(old, jnp.max(logits, axis=1, keepdims=True))
                terms = jnp.sum(jnp.exp(logits - new[:, 0:1]), axis=1, keepdims=True)
                mass[here, :] = mass[here, :] * jnp.exp(old - new) + terms
                top[here, :] = new

            log_rows[:, cells(s)] = jnp.transpose(top[...] + jnp.log(mass[...]))[0:1, :]


def general_columns(
    meta, own, base, x, ys, cs, x_block, y_block, c_block, weight, column, col_top, col_mass
):
    @pl.loop(0, MOST)
    def _(p):
        valid, s, side, t = place(meta, p)
        wanted = (side == 0) == own

        @pl.when(valid & wanted)
        def _():
            fetch(meta, p, x, ys, cs, x_block, y_block, c_block)
            column[...] = jnp.transpose(jnp.broadcast_to(weight[:, cells(s)], (128, BLK)))
            slot = base(side, t)

            @pl.loop(0, BLK // STEP)
            def _(q):
                here = pl.ds(pl.multiple_of(q * STEP, STEP), STEP)
                logits = products(x_block, q * STEP, y_block) + c_block[...] + column[here, 0:1]
                old = col_top[slot]
                new = jnp.maximum(old, jnp.max(logits, axis=0, keepdims=True))
                terms = jnp.sum(jnp.exp(logits - new[0:1, :]), axis=0, keepdims=True)
                col_mass[slot] = col_mass[slot] * jnp.exp(old - new) + terms
                col_top[slot] = new


def spill_out(spill, slots, sems, n):
    here = lax.rem(n, slots.shape[0])
    return pltpu.make_async_copy(slots.at[here], spill.at[n], sems.at[here])


def spill_in(spill, slots, sems, n):
    here = lax.rem(n, slots.shape[0])
    return pltpu.make_async_copy(spill.at[n], slots.at[here], sems.at[here])


def own_rows_kernel(
    meta, x, y, xt, keep, spill, total, c, norm, rows, ya, sums, slots, sems
):
    blocks = sums.shape[0]
    for s in range(blocks):
        norm[:, s * BLK : (s + 1) * BLK] = norms(x, s)
        doubled = 2.0 * x[:, s * BLK : (s + 1) * BLK].astype(f32)
        xt[s, :, 0:W] = jnp.transpose(doubled).astype(bf16)
        xt[s, :, W:DEPTH] = jnp.ones((BLK, DEPTH - W), bf16)
    fill_offsets(y, c)
    fill_targets(y, c, ya)
    sums[...] = jnp.zeros_like(sums)
    (count,) = list_rows(meta, (0, rows))
    kept = jnp.minimum(count, KEEP_OWN)
    row_pairs(meta, rows, kept, xt, ya, sums, keep, KEEP_OWN)
    extra = count - kept

    @pl.loop(0, extra)
    def _(n):
        @pl.when(n >= slots.shape[0])
        def _():
            spill_out(spill, slots, sems, n - slots.shape[0]).wait()

        _, s, _, t = place(meta, rows[kept + n])
        kernel_values(xt, ya, s, t, sums, slots, lax.rem(n, slots.shape[0]))
        spill_out(spill, slots, sems, n).start()

    @pl.loop(jnp.maximum(extra - slots.shape[0], 0), extra)
    def _(n):
        spill_out(spill, slots, sems, n).wait()

    for s in range(blocks):
        total[:, s * BLK : (s + 1) * BLK] = lane_sums(sums[s])


def near_rows_kernel(meta, xt, y, own_total, keep, total, c, rows, ya, sums):
    fill_offsets(y, c)
    fill_targets(y, c, ya)
    sums[...] = jnp.zeros_like(sums)
    (count,) = list_rows(meta, (near_side(meta), rows))
    row_pairs(meta, rows, count, xt, ya, sums, keep, KEEP_NEAR)
    for s in range(sums.shape[0]):
        here = slice(s * BLK, (s + 1) * BLK)
        total[:, here] = own_total[:, here] + lane_sums(sums[s])


def settle_kernel(
    meta, xt, x, y_near, c_near, y_own, c_own, y_far, norm, near_total, keep_near, log_src,
    potential, send_near, send_far, u, weight, fits, no_far,
    rows_near, rows_far, potential_row, potential_sem, c_far, ya, keep, sums, totals,
    x_block, y_block, c_block, col_top, col_mass,
):
    blocks = u.shape[0]
    top, mass, column = sums.at[0], sums.at[1], sums.at[2]
    fill_offsets(y_far, c_far)
    fill_targets(y_far, c_far, ya)
    sums[...] = jnp.zeros_like(sums)
    near = near_side(meta)
    count_near, count_far = list_rows(meta, (near, rows_near), (-near, rows_far))
    row_pairs(meta, rows_far, count_far, xt, ya, sums, keep, KEEP_FAR)

    lowest = jnp.minimum(jnp.minimum(c_near[...], c_far[...]), c_own[...])
    x2 = jnp.max(norm[...], axis=1, keepdims=True)
    c_min = jnp.min(lowest, axis=1, keepdims=True)
    y2 = jnp.maximum(10.0 - c_min, 0.0)
    extent = x2 + 10.0 + 2.0 * jnp.sqrt(x2) * jnp.sqrt(y2) - c_min
    in_range = jnp.max(extent) <= SPAN
    alone = (meta[0] == 0) | (meta[0] == meta[2] - 1)
    no_far[...] = jnp.full_like(no_far, jnp.where(alone, FLOOR, 0.0))
    fits[...] = jnp.broadcast_to(jnp.where(extent <= SPAN, 1.0, 0.0), fits.shape)
    offset = lambda side, t: jnp.where(side == near, t, blocks + t)

    @pl.when(in_range)
    def _():
        index = lax.broadcasted_iota(jnp.int32, (8, BLK), 0)
        for s in range(blocks):
            here = slice(s * BLK, (s + 1) * BLK)
            total = near_total[:, here] + lane_sums(sums[s])
            w = log_src[:, here] - jnp.log(total)
            weight[:, here] = w
            value = jnp.exp(w)
            high = value.astype(bf16).astype(f32)
            u[s] = jnp.where(index == 0, high, jnp.where(index == 1, value - high, 0.0))
        potential_row[...] = 0.5 * (weight[...] + norm[...])
        hand_over = pltpu.make_async_copy(potential_row, potential, potential_sem)
        hand_over.start()
        totals[...] = jnp.zeros_like(totals)
        column_pairs(
            meta, rows_far, count_far, xt, ya, u, keep, KEEP_FAR,
            keep, KEEP_FAR, totals, blocks,
        )

        @pl.when(count_near > KEEP_NEAR)
        def _():
            refill_targets(y_near, c_near, ya)

        column_pairs(
            meta, rows_near, count_near, xt, ya, u, keep_near, KEEP_NEAR,
            keep, KEEP_FAR, totals, 0,
        )
        for t in range(blocks):
            here = slice(t * BLK, (t + 1) * BLK)
            send_near[:, here] = logs(jnp.sum(totals[t], axis=0, keepdims=True))
            send_far[:, here] = logs(jnp.sum(totals[blocks + t], axis=0, keepdims=True))
        hand_over.wait()

    @pl.when(jnp.logical_not(in_range))
    def _():
        ys = (y_near, y_own, y_far)
        cs = (c_near, c_own, c_far)
        general_rows(meta, x, ys, cs, x_block, y_block, c_block, top, mass, weight)
        weight[...] = log_src[...] - weight[...]
        u[...] = jnp.zeros_like(u)
        col_top[...] = jnp.full_like(col_top, FLOOR)
        col_mass[...] = jnp.zeros_like(col_mass)
        general_columns(
            meta, False, offset, x, ys, cs, x_block, y_block, c_block, weight, column,
            col_top, col_mass,
        )
        for t in range(blocks):
            here = slice(t * BLK, (t + 1) * BLK)
            send_near[:, here] = (col_top[t] + logs(col_mass[t]))[0:1, :]
            send_far[:, here] = (col_top[blocks + t] + logs(col_mass[blocks + t]))[0:1, :]
        potential_row[...] = 0.5 * (weight[...] + norm[...])
        pltpu.sync_copy(potential_row, potential)


def own_columns_kernel(
    meta, x, y, c, keep, spill, u, weight, fits,
    out,
    rows, slots, sems, totals, x_block, y_block, c_block, column, col_top, col_mass,
):
    blocks = u.shape[0]
    in_range = jnp.max(fits[...]) > 0.5
    (count,) = list_rows(meta, (0, rows))

    @pl.when(in_range)
    def _():
        kept = jnp.minimum(count, KEEP_OWN)
        extra = count - kept

        @pl.loop(0, jnp.minimum(extra, slots.shape[0]))
        def _(n):
            spill_in(spill, slots, sems, n).start()

        totals[...] = jnp.zeros_like(totals)
        column_pairs(meta, rows, kept, None, None, u, keep, KEEP_OWN, None, 0, totals, 0)

        @pl.loop(0, extra)
        def _(n):
            spill_in(spill, slots, sems, n).wait()
            _, s, _, t = place(meta, rows[kept + n])
            values = slots[lax.rem(n, slots.shape[0])]
            totals[t] += jnp.dot(u[s].astype(bf16), values, preferred_element_type=f32)

            @pl.when(n + slots.shape[0] < extra)
            def _():
                spill_in(spill, slots, sems, n + slots.shape[0]).start()

        for t in range(blocks):
            out[:, t * BLK : (t + 1) * BLK] = logs(jnp.sum(totals[t], axis=0, keepdims=True))

    @pl.when(jnp.logical_not(in_range))
    def _():
        col_top[...] = jnp.full_like(col_top, FLOOR)
        col_mass[...] = jnp.zeros_like(col_mass)
        general_columns(
            meta, True, lambda side, t: t, x, (None, y, None), (None, c, None),
            x_block, y_block, c_block, weight, column, col_top, col_mass,
        )
        for t in range(blocks):
            here = slice(t * BLK, (t + 1) * BLK)
            out[:, here] = (col_top[t] + logs(col_mass[t]))[0:1, :]


def call(kernel, operands, outs, scratch, limit, pairs, outside=(), outside_outs=()):
    in_vmem = pl.BlockSpec(memory_space=pltpu.VMEM)
    in_smem = pl.BlockSpec(memory_space=pltpu.SMEM)
    anywhere = pl.BlockSpec(memory_space=pl.ANY)
    return pl.pallas_call(
        kernel,
        out_shape=outs,
        in_specs=[in_smem]
        + [anywhere if n in outside else in_vmem for n in range(1, len(operands))],
        out_specs=tuple(
            anywhere if out in outside_outs else in_vmem for out in range(len(outs))
        ),
        scratch_shapes=scratch,
        compiler_params=pltpu.CompilerParams(vmem_limit_bytes=limit << 20),
        cost_estimate=pl.CostEstimate(
            flops=pairs * 2 * BLK * BLK * 256, bytes_accessed=1 << 20, transcendentals=pairs * BLK * BLK
        ),
    )(*operands)


def on_device(source_emb, target_emb, target_pot, log_src, log_tgt, pair_list):
    position = lax.axis_index(AXES)
    width = source_emb.shape[1]
    blocks = width // BLK
    row = jax.ShapeDtypeStruct((1, width), f32)
    pots = target_pot.reshape(width // 128, 128)
    pots = jnp.pad(pots, ((0, W - width // 128), (0, 0)))
    packed = jnp.concatenate([target_emb, pots], axis=1)
    from_near = swapped(packed, True)
    from_far = swapped(packed, False)
    twice = 2.0 * target_pot.astype(f32)

    mine = lax.dynamic_slice_in_dim(pair_list, position * P_DEV, MOST, 0)
    meta = jnp.concatenate(
        [jnp.stack([position, jnp.int32(blocks), jnp.int32(lax.axis_size(AXES))]).astype(jnp.int32), mine[:, 0], mine[:, 1]]
    )

    def kept(n):
        return pltpu.VMEM((n, BLK, BLK), bf16)

    sums_shape = (blocks, BLK, 128)
    ya_shape = pltpu.VMEM((blocks, DEPTH, BLK), bf16)
    rows_shape = pltpu.SMEM((MOST + 1,), jnp.int32)
    row_here = pltpu.VMEM((1, width), f32)
    xt, keep_own, spill, own_total, c_own, norm = call(
        own_rows_kernel,
        (meta, source_emb, packed),
        (pltpu.VMEM((blocks, BLK, DEPTH), bf16), kept(KEEP_OWN),
         jax.ShapeDtypeStruct((MOST - KEEP_OWN, BLK, BLK), bf16), row_here, row_here, row_here),
        [rows_shape, ya_shape, pltpu.VMEM(sums_shape, f32), kept(2), pltpu.SemaphoreType.DMA((2,))],
        LIMITS[0],
        9,
        (),
        (2,),
    )
    keep_near, near_total, c_near = call(
        near_rows_kernel,
        (meta, xt, from_near, own_total),
        (kept(KEEP_NEAR), row_here, row_here),
        [rows_shape, ya_shape, pltpu.VMEM(sums_shape, f32)],
        LIMITS[1],
        4,
    )
    block_scratch = [pltpu.VMEM((W, BLK), bf16)] * 2 + [pltpu.VMEM((1, BLK), f32)]
    wide = pltpu.VMEM((BLK, 128), f32)
    one = jax.ShapeDtypeStruct((1, 128), f32)
    potential, send_near, send_far, u, weight, fits, no_far = call(
        settle_kernel,
        (meta, xt, source_emb, from_near, c_near, target_emb, c_own, from_far, norm,
         near_total, keep_near, log_src.reshape(1, width)),
        (row, row, row, pltpu.VMEM((blocks, 8, BLK), f32), row, one, row_here),
        [rows_shape, rows_shape, row_here, pltpu.SemaphoreType.DMA, row_here, ya_shape, kept(KEEP_FAR + 1),
         pltpu.VMEM(sums_shape, f32), pltpu.VMEM((2 * blocks, 8, BLK), f32)] + block_scratch
        + [pltpu.VMEM((2 * blocks, 1, BLK), f32)] * 2,
        LIMITS[2],
        8,
        (2, 3, 5),
        (0,),
    )
    got_far = swapped(send_far, False)
    got_near = swapped(send_near, True)
    (own,) = call(
        own_columns_kernel,
        (meta, source_emb, target_emb, c_own, keep_own, spill, u, weight, fits),
        (row,),
        [rows_shape, kept(SLOTS), pltpu.SemaphoreType.DMA((SLOTS,)), pltpu.VMEM((blocks, 8, BLK), f32)] + block_scratch + [wide]
        + [pltpu.VMEM((blocks, 1, BLK), f32)] * 2,
        LIMITS[3],
        6,
        (1, 2, 5),
    )
    got_far = (got_far + no_far).reshape(width)
    got_near = got_near.reshape(width)
    own = own.reshape(width)
    top = jnp.maximum(jnp.maximum(got_far, got_near), own)
    total = jnp.exp(got_far - top) + jnp.exp(got_near - top) + jnp.exp(own - top)
    target_potential = 0.5 * (log_tgt + twice - (top + jnp.log(total)))
    return potential.reshape(width), target_potential


def solution(mesh):
    return jax.shard_map(
        on_device,
        mesh=mesh,
        in_specs=(P(None, AXES), P(None, AXES), P(AXES), P(AXES), P(AXES), P()),
        out_specs=(P(AXES), P(AXES)),
        check_vma=False,
    )
```

```python
import functools

import jax
import jax.numpy as jnp
from jax import lax
from jax.experimental import pallas as pl
from jax.experimental.pallas import tpu as pltpu
from jax.sharding import PartitionSpec as P

BLK = 1024
P_DEV = 18
W = 64
DEPTH = 80
MOST = 21
KEEP_OWN = 7
KEEP_NEAR = 7
KEEP_FAR = 8
SLOTS = 4
FLOOR = -1.0e30
SPAN = 75.0
ROWS = 256
LIMITS = (10, 6, 25, 12)
AXES = ("grp", "dev")
f32 = jnp.float32
bf16 = jnp.bfloat16


def swapped(value, near):
    count = lax.axis_size(AXES)
    pairs = [(i, i + 1) for i in range(0 if near else 1, count - 1, 2)]
    return lax.ppermute(value, AXES, pairs + [(j, i) for i, j in pairs])


def near_side(meta):
    return 1 - 2 * (meta[0] & 1)


def place(meta, p):
    device = meta[0]
    blocks = meta[1]
    source = meta[3 + p] - device * blocks
    target = meta[3 + MOST + p] - device * blocks
    valid = (source >= 0) & (source < blocks)
    side = jnp.where(target < 0, -1, jnp.where(target >= blocks, 1, 0))
    return valid, jnp.clip(source, 0, blocks - 1), side, target - side * blocks


def list_rows(meta, *wanted):
    counts = [jnp.int32(0)] * len(wanted)
    for p in range(MOST):
        valid, _, side, _ = place(meta, p)
        for n, (side_wanted, rows) in enumerate(wanted):
            rows[counts[n]] = p
            counts[n] = counts[n] + (valid & (side == side_wanted)).astype(jnp.int32)
    return counts


def cells(block):
    return pl.ds(pl.multiple_of(block * BLK, BLK), BLK)


def some_at_a_time(start, stop, body):
    fours = lax.shift_right_logical(stop - start, jnp.int32(2))
    rest = start + 4 * fours

    @pl.loop(0, fours)
    def _(n):
        for m in range(4):
            body(start + 4 * n + m)

    @pl.when(((stop - start) & 2) != 0)
    def _():
        body(rest)
        body(rest + 1)

    @pl.when(((stop - start) & 1) != 0)
    def _():
        body(stop - 1)


def fill_offsets(y, c):
    width = c.shape[1]
    pots = y[:, width : width + 128].astype(f32)
    for t in range(width // BLK):
        rows = range(t * (BLK // 128), (t + 1) * (BLK // 128))
        row = jnp.concatenate([pots[r : r + 1, :] for r in rows], axis=1)
        c[:, t * BLK : (t + 1) * BLK] = 2.0 * row - norms(y, t)


def fill_targets(y, c, ya):
    for t in range(ya.shape[0]):
        ya[t, 0:W, :] = y[:, t * BLK : (t + 1) * BLK]
    fill_rows(c, ya)


def refill_targets(y, c, ya):
    for t in range(ya.shape[0]):
        pltpu.sync_copy(y.at[:, pl.ds(t * BLK, BLK)], ya.at[t, pl.ds(0, W), :])
    fill_rows(c, ya)


def fill_rows(c, ya):
    for t in range(ya.shape[0]):
        row = c[:, t * BLK : (t + 1) * BLK]
        high = row.astype(bf16).astype(f32)
        rest = row - high
        middle = rest.astype(bf16).astype(f32)
        low = rest - middle
        index = lax.broadcasted_iota(jnp.int32, (DEPTH - W, BLK), 0)
        extra = jnp.where(
            index == 0, high, jnp.where(index == 1, middle, jnp.where(index == 2, low, 0.0))
        )
        ya[t, W:DEPTH, :] = extra.astype(bf16)


def kernel_values(xt, ya, s, t, sums, keep, slot):
    for first in range(0, BLK, ROWS):
        here = pl.ds(first, ROWS)
        k = jnp.exp(jnp.dot(xt[s, here, :], ya[t], preferred_element_type=f32))
        if sums is not None:
            part = k[:, 0:128]
            for j in range(128, BLK, 128):
                part = part + k[:, j : j + 128]
            sums[s, here, :] += part
        if keep is not None:
            keep[slot, here, :] = k.astype(bf16)


def row_pairs(meta, rows, count, xt, ya, sums, keep, capacity):
    def kept(n):
        _, s, _, t = place(meta, rows[n])
        kernel_values(xt, ya, s, t, sums, keep, n)

    some_at_a_time(0, jnp.minimum(count, capacity), kept)

    @pl.loop(jnp.minimum(count, capacity), count)
    def _(n):
        _, s, _, t = place(meta, rows[n])
        kernel_values(xt, ya, s, t, sums, None, 0)


def column_pairs(meta, rows, count, xt, ya, u, keep, capacity, spare, spare_slot, totals, base):
    def add(s, t, k):
        totals[base + t] += jnp.dot(u[s].astype(bf16), k, preferred_element_type=f32)

    def kept(n):
        _, s, _, t = place(meta, rows[n])
        add(s, t, keep[n])

    some_at_a_time(0, jnp.minimum(count, capacity), kept)

    if spare is None:
        return

    @pl.loop(jnp.minimum(count, capacity), count)
    def _(n):
        _, s, _, t = place(meta, rows[n])
        kernel_values(xt, ya, s, t, None, spare, spare_slot)
        add(s, t, spare[spare_slot])


def lane_sums(part):
    return jnp.sum(jnp.transpose(part), axis=0, keepdims=True)


def norms(x, s):
    full = x[:, s * BLK : (s + 1) * BLK].astype(f32)
    return jnp.sum(full * full, axis=0, keepdims=True)


def logs(total):
    return jnp.where(total > 0.0, jnp.log(jnp.where(total > 0.0, total, 1.0)), FLOOR)


STEP = 128


def fetch(meta, p, x, ys, cs, x_block, y_block, c_block):
    _, s, side, t = place(meta, p)
    pltpu.sync_copy(x.at[:, cells(s)], x_block)
    near = near_side(meta)
    for side_here, y, c in zip((near, 0, -near), ys, cs):
        if y is None:
            continue

        @pl.when(side == side_here)
        def _():
            pltpu.sync_copy(y.at[:, cells(t)], y_block)
            c_block[...] = c[:, cells(t)]


def products(x_block, first, y_block):
    x_part = x_block[:, pl.ds(pl.multiple_of(first, STEP), STEP)]
    return 2.0 * lax.dot_general(
        x_part, y_block[...], (((0,), (0,)), ((), ())), preferred_element_type=f32
    )


def general_rows(meta, x, ys, cs, x_block, y_block, c_block, top, mass, log_rows):
    @pl.loop(0, MOST)
    def _(p):
        valid, s, _, _ = place(meta, p)
        before_valid, before, _, _ = place(meta, jnp.maximum(p - 1, 0))

        @pl.when(valid)
        def _():
            @pl.when((p == 0) | jnp.logical_not(before_valid) | (before != s))
            def _():
                top[...] = jnp.full_like(top, FLOOR)
                mass[...] = jnp.zeros_like(mass)

            fetch(meta, p, x, ys, cs, x_block, y_block, c_block)

            @pl.loop(0, BLK // STEP)
            def _(q):
                here = pl.ds(pl.multiple_of(q * STEP, STEP), STEP)
                logits = products(x_block, q * STEP, y_block) + c_block[...]
                old = top[here, :]
                new = jnp.maximum(old, jnp.max(logits, axis=1, keepdims=True))
                terms = jnp.sum(jnp.exp(logits - new[:, 0:1]), axis=1, keepdims=True)
                mass[here, :] = mass[here, :] * jnp.exp(old - new) + terms
                top[here, :] = new

            log_rows[:, cells(s)] = jnp.transpose(top[...] + jnp.log(mass[...]))[0:1, :]


def general_columns(
    meta, own, base, x, ys, cs, x_block, y_block, c_block, weight, column, col_top, col_mass
):
    @pl.loop(0, MOST)
    def _(p):
        valid, s, side, t = place(meta, p)
        wanted = (side == 0) == own

        @pl.when(valid & wanted)
        def _():
            fetch(meta, p, x, ys, cs, x_block, y_block, c_block)
            column[...] = jnp.transpose(jnp.broadcast_to(weight[:, cells(s)], (128, BLK)))
            slot = base(side, t)

            @pl.loop(0, BLK // STEP)
            def _(q):
                here = pl.ds(pl.multiple_of(q * STEP, STEP), STEP)
                logits = products(x_block, q * STEP, y_block) + c_block[...] + column[here, 0:1]
                old = col_top[slot]
                new = jnp.maximum(old, jnp.max(logits, axis=0, keepdims=True))
                terms = jnp.sum(jnp.exp(logits - new[0:1, :]), axis=0, keepdims=True)
                col_mass[slot] = col_mass[slot] * jnp.exp(old - new) + terms
                col_top[slot] = new


def spill_out(spill, slots, sems, n):
    here = lax.rem(n, slots.shape[0])
    return pltpu.make_async_copy(slots.at[here], spill.at[n], sems.at[here])


def spill_in(spill, slots, sems, n):
    here = lax.rem(n, slots.shape[0])
    return pltpu.make_async_copy(spill.at[n], slots.at[here], sems.at[here])


def own_rows_kernel(
    meta, x, y, xt, keep, spill, total, c, norm, rows, ya, sums, slots, sems
):
    blocks = sums.shape[0]
    for s in range(blocks):
        norm[:, s * BLK : (s + 1) * BLK] = norms(x, s)
        doubled = 2.0 * x[:, s * BLK : (s + 1) * BLK].astype(f32)
        xt[s, :, 0:W] = jnp.transpose(doubled).astype(bf16)
        xt[s, :, W:DEPTH] = jnp.ones((BLK, DEPTH - W), bf16)
    fill_offsets(y, c)
    fill_targets(y, c, ya)
    sums[...] = jnp.zeros_like(sums)
    (count,) = list_rows(meta, (0, rows))
    kept = jnp.minimum(count, KEEP_OWN)
    row_pairs(meta, rows, kept, xt, ya, sums, keep, KEEP_OWN)
    extra = count - kept

    @pl.loop(0, extra)
    def _(n):
        @pl.when(n >= slots.shape[0])
        def _():
            spill_out(spill, slots, sems, n - slots.shape[0]).wait()

        _, s, _, t = place(meta, rows[kept + n])
        kernel_values(xt, ya, s, t, sums, slots, lax.rem(n, slots.shape[0]))
        spill_out(spill, slots, sems, n).start()

    @pl.loop(jnp.maximum(extra - slots.shape[0], 0), extra)
    def _(n):
        spill_out(spill, slots, sems, n).wait()

    for s in range(blocks):
        total[:, s * BLK : (s + 1) * BLK] = lane_sums(sums[s])


def near_rows_kernel(meta, xt, y, own_total, keep, total, c, rows, ya, sums):
    fill_offsets(y, c)
    fill_targets(y, c, ya)
    sums[...] = jnp.zeros_like(sums)
    (count,) = list_rows(meta, (near_side(meta), rows))
    row_pairs(meta, rows, count, xt, ya, sums, keep, KEEP_NEAR)
    for s in range(sums.shape[0]):
        here = slice(s * BLK, (s + 1) * BLK)
        total[:, here] = own_total[:, here] + lane_sums(sums[s])


def settle_kernel(
    meta, xt, x, y_near, c_near, y_own, c_own, y_far, norm, near_total, keep_near, log_src,
    potential, send_near, send_far, u, weight, fits, no_far,
    rows_near, rows_far, potential_row, potential_sem, c_far, ya, keep, sums, totals,
    x_block, y_block, c_block, col_top, col_mass,
):
    blocks = u.shape[0]
    top, mass, column = sums.at[0], sums.at[1], sums.at[2]
    fill_offsets(y_far, c_far)
    fill_targets(y_far, c_far, ya)
    sums[...] = jnp.zeros_like(sums)
    near = near_side(meta)
    count_near, count_far = list_rows(meta, (near, rows_near), (-near, rows_far))
    row_pairs(meta, rows_far, count_far, xt, ya, sums, keep, KEEP_FAR)

    lowest = jnp.minimum(jnp.minimum(c_near[...], c_far[...]), c_own[...])
    x2 = jnp.max(norm[...], axis=1, keepdims=True)
    c_min = jnp.min(lowest, axis=1, keepdims=True)
    y2 = jnp.maximum(10.0 - c_min, 0.0)
    extent = x2 + 10.0 + 2.0 * jnp.sqrt(x2) * jnp.sqrt(y2) - c_min
    in_range = jnp.max(extent) <= SPAN
    alone = (meta[0] == 0) | (meta[0] == meta[2] - 1)
    no_far[...] = jnp.full_like(no_far, jnp.where(alone, FLOOR, 0.0))
    fits[...] = jnp.broadcast_to(jnp.where(extent <= SPAN, 1.0, 0.0), fits.shape)
    offset = lambda side, t: jnp.where(side == near, t, blocks + t)

    @pl.when(in_range)
    def _():
        index = lax.broadcasted_iota(jnp.int32, (8, BLK), 0)
        for s in range(blocks):
            here = slice(s * BLK, (s + 1) * BLK)
            total = near_total[:, here] + lane_sums(sums[s])
            w = log_src[:, here] - jnp.log(total)
            weight[:, here] = w
            value = jnp.exp(w)
            high = value.astype(bf16).astype(f32)
            u[s] = jnp.where(index == 0, high, jnp.where(index == 1, value - high, 0.0))
        potential_row[...] = 0.5 * (weight[...] + norm[...])
        hand_over = pltpu.make_async_copy(potential_row, potential, potential_sem)
        hand_over.start()
        totals[...] = jnp.zeros_like(totals)
        column_pairs(
            meta, rows_far, count_far, xt, ya, u, keep, KEEP_FAR,
            keep, KEEP_FAR, totals, blocks,
        )

        @pl.when(count_near > KEEP_NEAR)
        def _():
            refill_targets(y_near, c_near, ya)

        column_pairs(
            meta, rows_near, count_near, xt, ya, u, keep_near, KEEP_NEAR,
            keep, KEEP_FAR, totals, 0,
        )
        for t in range(blocks):
            here = slice(t * BLK, (t + 1) * BLK)
            send_near[:, here] = logs(jnp.sum(totals[t], axis=0, keepdims=True))
            send_far[:, here] = logs(jnp.sum(totals[blocks + t], axis=0, keepdims=True))
        hand_over.wait()

    @pl.when(jnp.logical_not(in_range))
    def _():
        ys = (y_near, y_own, y_far)
        cs = (c_near, c_own, c_far)
        general_rows(meta, x, ys, cs, x_block, y_block, c_block, top, mass, weight)
        weight[...] = log_src[...] - weight[...]
        u[...] = jnp.zeros_like(u)
        col_top[...] = jnp.full_like(col_top, FLOOR)
        col_mass[...] = jnp.zeros_like(col_mass)
        general_columns(
            meta, False, offset, x, ys, cs, x_block, y_block, c_block, weight, column,
            col_top, col_mass,
        )
        for t in range(blocks):
            here = slice(t * BLK, (t + 1) * BLK)
            send_near[:, here] = (col_top[t] + logs(col_mass[t]))[0:1, :]
            send_far[:, here] = (col_top[blocks + t] + logs(col_mass[blocks + t]))[0:1, :]
        potential_row[...] = 0.5 * (weight[...] + norm[...])
        pltpu.sync_copy(potential_row, potential)


def own_columns_kernel(
    meta, x, y, c, keep, spill, u, weight, fits,
    out,
    rows, slots, sems, totals, x_block, y_block, c_block, column, col_top, col_mass,
):
    blocks = u.shape[0]
    in_range = jnp.max(fits[...]) > 0.5
    (count,) = list_rows(meta, (0, rows))

    @pl.when(in_range)
    def _():
        kept = jnp.minimum(count, KEEP_OWN)
        extra = count - kept

        @pl.loop(0, jnp.minimum(extra, slots.shape[0]))
        def _(n):
            spill_in(spill, slots, sems, n).start()

        totals[...] = jnp.zeros_like(totals)
        column_pairs(meta, rows, kept, None, None, u, keep, KEEP_OWN, None, 0, totals, 0)

        @pl.loop(0, extra)
        def _(n):
            spill_in(spill, slots, sems, n).wait()
            _, s, _, t = place(meta, rows[kept + n])
            values = slots[lax.rem(n, slots.shape[0])]
            totals[t] += jnp.dot(u[s].astype(bf16), values, preferred_element_type=f32)

            @pl.when(n + slots.shape[0] < extra)
            def _():
                spill_in(spill, slots, sems, n + slots.shape[0]).start()

        for t in range(blocks):
            out[:, t * BLK : (t + 1) * BLK] = logs(jnp.sum(totals[t], axis=0, keepdims=True))

    @pl.when(jnp.logical_not(in_range))
    def _():
        col_top[...] = jnp.full_like(col_top, FLOOR)
        col_mass[...] = jnp.zeros_like(col_mass)
        general_columns(
            meta, True, lambda side, t: t, x, (None, y, None), (None, c, None),
            x_block, y_block, c_block, weight, column, col_top, col_mass,
        )
        for t in range(blocks):
            here = slice(t * BLK, (t + 1) * BLK)
            out[:, here] = (col_top[t] + logs(col_mass[t]))[0:1, :]


def call(kernel, operands, outs, scratch, limit, pairs, outside=(), outside_outs=()):
    in_vmem = pl.BlockSpec(memory_space=pltpu.VMEM)
    in_smem = pl.BlockSpec(memory_space=pltpu.SMEM)
    anywhere = pl.BlockSpec(memory_space=pl.ANY)
    return pl.pallas_call(
        kernel,
        out_shape=outs,
        in_specs=[in_smem]
        + [anywhere if n in outside else in_vmem for n in range(1, len(operands))],
        out_specs=tuple(
            anywhere if out in outside_outs else in_vmem for out in range(len(outs))
        ),
        scratch_shapes=scratch,
        compiler_params=pltpu.CompilerParams(vmem_limit_bytes=limit << 20),
        cost_estimate=pl.CostEstimate(
            flops=pairs * 2 * BLK * BLK * 256, bytes_accessed=1 << 20, transcendentals=pairs * BLK * BLK
        ),
    )(*operands)


def on_device(source_emb, target_emb, target_pot, log_src, log_tgt, pair_list):
    position = lax.axis_index(AXES)
    width = source_emb.shape[1]
    blocks = width // BLK
    row = jax.ShapeDtypeStruct((1, width), f32)
    first, target_emb = lax.optimization_barrier((position * P_DEV, target_emb))
    pots = target_pot.reshape(width // 128, 128)
    pots = jnp.pad(pots, ((0, W - width // 128), (0, 0)))
    packed = jnp.concatenate([target_emb, pots], axis=1)
    from_near = swapped(packed, True)
    from_far = swapped(packed, False)
    twice = 2.0 * target_pot.astype(f32)

    mine = lax.dynamic_slice_in_dim(pair_list, first, MOST, 0, allow_negative_indices=False)
    meta = jnp.concatenate(
        [jnp.stack([position, jnp.int32(blocks), jnp.int32(lax.axis_size(AXES))]).astype(jnp.int32), mine[:, 0], mine[:, 1]]
    )

    def kept(n):
        return pltpu.VMEM((n, BLK, BLK), bf16)

    sums_shape = (blocks, BLK, 128)
    ya_shape = pltpu.VMEM((blocks, DEPTH, BLK), bf16)
    rows_shape = pltpu.SMEM((MOST + 1,), jnp.int32)
    row_here = pltpu.VMEM((1, width), f32)
    xt, keep_own, spill, own_total, c_own, norm = call(
        own_rows_kernel,
        (meta, source_emb, packed),
        (pltpu.VMEM((blocks, BLK, DEPTH), bf16), kept(KEEP_OWN),
         jax.ShapeDtypeStruct((MOST - KEEP_OWN, BLK, BLK), bf16), row_here, row_here, row_here),
        [rows_shape, ya_shape, pltpu.VMEM(sums_shape, f32), kept(2), pltpu.SemaphoreType.DMA((2,))],
        LIMITS[0],
        9,
        (),
        (2,),
    )
    keep_near, near_total, c_near = call(
        near_rows_kernel,
        (meta, xt, from_near, own_total),
        (kept(KEEP_NEAR), row_here, row_here),
        [rows_shape, ya_shape, pltpu.VMEM(sums_shape, f32)],
        LIMITS[1],
        4,
    )
    block_scratch = [pltpu.VMEM((W, BLK), bf16)] * 2 + [pltpu.VMEM((1, BLK), f32)]
    wide = pltpu.VMEM((BLK, 128), f32)
    one = jax.ShapeDtypeStruct((1, 128), f32)
    potential, send_near, send_far, u, weight, fits, no_far = call(
        settle_kernel,
        (meta, xt, source_emb, from_near, c_near, target_emb, c_own, from_far, norm,
         near_total, keep_near, log_src.reshape(1, width)),
        (row, row, row, pltpu.VMEM((blocks, 8, BLK), f32), row, one, row_here),
        [rows_shape, rows_shape, row_here, pltpu.SemaphoreType.DMA, row_here, ya_shape, kept(KEEP_FAR + 1),
         pltpu.VMEM(sums_shape, f32), pltpu.VMEM((2 * blocks, 8, BLK), f32)] + block_scratch
        + [pltpu.VMEM((2 * blocks, 1, BLK), f32)] * 2,
        LIMITS[2],
        8,
        (2, 3, 5),
        (0,),
    )
    got_far = swapped(send_far, False)
    got_near = swapped(send_near, True)
    (own,) = call(
        own_columns_kernel,
        (meta, source_emb, target_emb, c_own, keep_own, spill, u, weight, fits),
        (row,),
        [rows_shape, kept(SLOTS), pltpu.SemaphoreType.DMA((SLOTS,)), pltpu.VMEM((blocks, 8, BLK), f32)] + block_scratch + [wide]
        + [pltpu.VMEM((blocks, 1, BLK), f32)] * 2,
        LIMITS[3],
        6,
        (1, 2, 5),
    )
    got_far = (got_far + no_far).reshape(width)
    got_near = got_near.reshape(width)
    own = own.reshape(width)
    top = jnp.maximum(jnp.maximum(got_far, got_near), own)
    total = jnp.exp(got_far - top) + jnp.exp(got_near - top) + jnp.exp(own - top)
    target_potential = 0.5 * (log_tgt + twice - (top + jnp.log(total)))
    return potential.reshape(width), target_potential


def solution(mesh):
    return jax.shard_map(
        on_device,
        mesh=mesh,
        in_specs=(P(None, AXES), P(None, AXES), P(AXES), P(AXES), P(AXES), P()),
        out_specs=(P(AXES), P(AXES)),
        check_vma=False,
    )
```

```python
import functools

import jax
import jax.numpy as jnp
from jax import lax
from jax.experimental import pallas as pl
from jax.experimental.pallas import tpu as pltpu
from jax.sharding import PartitionSpec as P

BLK = 1024
P_DEV = 18
W = 64
DEPTH = 80
MOST = 21
KEEP_OWN = 7
KEEP_NEAR = 7
KEEP_FAR = 8
SLOTS = 6
FLOOR = -1.0e30
SPAN = 75.0
ROWS = 256
LIMITS = (10, 6, 25, 16)
AXES = ("grp", "dev")
f32 = jnp.float32
bf16 = jnp.bfloat16


def swapped(value, near):
    count = lax.axis_size(AXES)
    pairs = [(i, i + 1) for i in range(0 if near else 1, count - 1, 2)]
    return lax.ppermute(value, AXES, pairs + [(j, i) for i, j in pairs])


def near_side(meta):
    return 1 - 2 * (meta[0] & 1)


def place(meta, p):
    device = meta[0]
    blocks = meta[1]
    source = meta[3 + p] - device * blocks
    target = meta[3 + MOST + p] - device * blocks
    valid = (source >= 0) & (source < blocks)
    side = jnp.where(target < 0, -1, jnp.where(target >= blocks, 1, 0))
    return valid, jnp.clip(source, 0, blocks - 1), side, target - side * blocks


def list_rows(meta, *wanted):
    counts = [jnp.int32(0)] * len(wanted)
    for p in range(MOST):
        valid, _, side, _ = place(meta, p)
        for n, (side_wanted, rows) in enumerate(wanted):
            rows[counts[n]] = p
            counts[n] = counts[n] + (valid & (side == side_wanted)).astype(jnp.int32)
    return counts


def cells(block):
    return pl.ds(pl.multiple_of(block * BLK, BLK), BLK)


def two_at_a_time(start, stop, body):
    half = lax.shift_right_logical(stop - start, jnp.int32(1))

    @pl.loop(0, half)
    def _(n):
        body(start + 2 * n)
        body(start + 2 * n + 1)

    @pl.when(start + 2 * half < stop)
    def _():
        body(stop - 1)


def fill_offsets(y, c):
    width = c.shape[1]
    pots = y[:, width : width + 128].astype(f32)
    for t in range(width // BLK):
        rows = range(t * (BLK // 128), (t + 1) * (BLK // 128))
        row = jnp.concatenate([pots[r : r + 1, :] for r in rows], axis=1)
        c[:, t * BLK : (t + 1) * BLK] = 2.0 * row - norms(y, t)


def fill_targets(y, c, ya):
    for t in range(ya.shape[0]):
        ya[t, 0:W, :] = y[:, t * BLK : (t + 1) * BLK]
    fill_rows(c, ya)


def refill_targets(y, c, ya):
    for t in range(ya.shape[0]):
        pltpu.sync_copy(y.at[:, pl.ds(t * BLK, BLK)], ya.at[t, pl.ds(0, W), :])
    fill_rows(c, ya)


def fill_rows(c, ya):
    for t in range(ya.shape[0]):
        row = c[:, t * BLK : (t + 1) * BLK]
        high = row.astype(bf16).astype(f32)
        rest = row - high
        middle = rest.astype(bf16).astype(f32)
        low = rest - middle
        index = lax.broadcasted_iota(jnp.int32, (DEPTH - W, BLK), 0)
        extra = jnp.where(
            index == 0, high, jnp.where(index == 1, middle, jnp.where(index == 2, low, 0.0))
        )
        ya[t, W:DEPTH, :] = extra.astype(bf16)


def kernel_values(xt, ya, s, t, sums, keep, slot):
    for first in range(0, BLK, ROWS):
        here = pl.ds(first, ROWS)
        k = jnp.exp(jnp.dot(xt[s, here, :], ya[t], preferred_element_type=f32))
        if sums is not None:
            part = k[:, 0:128]
            for j in range(128, BLK, 128):
                part = part + k[:, j : j + 128]
            sums[s, here, :] += part
        if keep is not None:
            keep[slot, here, :] = k.astype(bf16)


def row_pairs(meta, rows, count, xt, ya, sums, keep, capacity):
    def kept(n):
        _, s, _, t = place(meta, rows[n])
        kernel_values(xt, ya, s, t, sums, keep, n)

    two_at_a_time(0, jnp.minimum(count, capacity), kept)

    @pl.loop(jnp.minimum(count, capacity), count)
    def _(n):
        _, s, _, t = place(meta, rows[n])
        kernel_values(xt, ya, s, t, sums, None, 0)


def column_pairs(meta, rows, count, xt, ya, u, keep, capacity, spare, spare_slot, totals, base):
    def add(s, t, k):
        totals[base + t] += jnp.dot(u[s].astype(bf16), k, preferred_element_type=f32)

    def kept(n):
        _, s, _, t = place(meta, rows[n])
        add(s, t, keep[n])

    two_at_a_time(0, jnp.minimum(count, capacity), kept)

    if spare is None:
        return

    @pl.loop(jnp.minimum(count, capacity), count)
    def _(n):
        _, s, _, t = place(meta, rows[n])
        kernel_values(xt, ya, s, t, None, spare, spare_slot)
        add(s, t, spare[spare_slot])


def lane_sums(part):
    return jnp.sum(jnp.transpose(part), axis=0, keepdims=True)


def norms(x, s):
    full = x[:, s * BLK : (s + 1) * BLK].astype(f32)
    return jnp.sum(full * full, axis=0, keepdims=True)


def logs(total):
    return jnp.where(total > 0.0, jnp.log(jnp.where(total > 0.0, total, 1.0)), FLOOR)


STEP = 128


def fetch(meta, p, x, ys, cs, x_block, y_block, c_block):
    _, s, side, t = place(meta, p)
    pltpu.sync_copy(x.at[:, cells(s)], x_block)
    near = near_side(meta)
    for side_here, y, c in zip((near, 0, -near), ys, cs):
        if y is None:
            continue

        @pl.when(side == side_here)
        def _():
            pltpu.sync_copy(y.at[:, cells(t)], y_block)
            c_block[...] = c[:, cells(t)]


def products(x_block, first, y_block):
    x_part = x_block[:, pl.ds(pl.multiple_of(first, STEP), STEP)]
    return 2.0 * lax.dot_general(
        x_part, y_block[...], (((0,), (0,)), ((), ())), preferred_element_type=f32
    )


def general_rows(meta, x, ys, cs, x_block, y_block, c_block, top, mass, log_rows):
    @pl.loop(0, MOST)
    def _(p):
        valid, s, _, _ = place(meta, p)
        before_valid, before, _, _ = place(meta, jnp.maximum(p - 1, 0))

        @pl.when(valid)
        def _():
            @pl.when((p == 0) | jnp.logical_not(before_valid) | (before != s))
            def _():
                top[...] = jnp.full_like(top, FLOOR)
                mass[...] = jnp.zeros_like(mass)

            fetch(meta, p, x, ys, cs, x_block, y_block, c_block)

            @pl.loop(0, BLK // STEP)
            def _(q):
                here = pl.ds(pl.multiple_of(q * STEP, STEP), STEP)
                logits = products(x_block, q * STEP, y_block) + c_block[...]
                old = top[here, :]
                new = jnp.maximum(old, jnp.max(logits, axis=1, keepdims=True))
                terms = jnp.sum(jnp.exp(logits - new[:, 0:1]), axis=1, keepdims=True)
                mass[here, :] = mass[here, :] * jnp.exp(old - new) + terms
                top[here, :] = new

            log_rows[:, cells(s)] = jnp.transpose(top[...] + jnp.log(mass[...]))[0:1, :]


def general_columns(
    meta, own, base, x, ys, cs, x_block, y_block, c_block, weight, column, col_top, col_mass
):
    @pl.loop(0, MOST)
    def _(p):
        valid, s, side, t = place(meta, p)
        wanted = (side == 0) == own

        @pl.when(valid & wanted)
        def _():
            fetch(meta, p, x, ys, cs, x_block, y_block, c_block)
            column[...] = jnp.transpose(jnp.broadcast_to(weight[:, cells(s)], (128, BLK)))
            slot = base(side, t)

            @pl.loop(0, BLK // STEP)
            def _(q):
                here = pl.ds(pl.multiple_of(q * STEP, STEP), STEP)
                logits = products(x_block, q * STEP, y_block) + c_block[...] + column[here, 0:1]
                old = col_top[slot]
                new = jnp.maximum(old, jnp.max(logits, axis=0, keepdims=True))
                terms = jnp.sum(jnp.exp(logits - new[0:1, :]), axis=0, keepdims=True)
                col_mass[slot] = col_mass[slot] * jnp.exp(old - new) + terms
                col_top[slot] = new


def spill_out(spill, slots, sems, n):
    here = lax.rem(n, slots.shape[0])
    return pltpu.make_async_copy(slots.at[here], spill.at[n], sems.at[here])


def spill_in(spill, slots, sems, n):
    here = lax.rem(n, slots.shape[0])
    return pltpu.make_async_copy(spill.at[n], slots.at[here], sems.at[here])


def own_rows_kernel(
    meta, x, y, xt, keep, spill, total, c, norm, rows, ya, sums, slots, sems
):
    blocks = sums.shape[0]
    for s in range(blocks):
        norm[:, s * BLK : (s + 1) * BLK] = norms(x, s)
        doubled = 2.0 * x[:, s * BLK : (s + 1) * BLK].astype(f32)
        xt[s, :, 0:W] = jnp.transpose(doubled).astype(bf16)
        xt[s, :, W:DEPTH] = jnp.ones((BLK, DEPTH - W), bf16)
    fill_offsets(y, c)
    fill_targets(y, c, ya)
    sums[...] = jnp.zeros_like(sums)
    (count,) = list_rows(meta, (0, rows))
    kept = jnp.minimum(count, KEEP_OWN)
    row_pairs(meta, rows, kept, xt, ya, sums, keep, KEEP_OWN)
    extra = count - kept

    @pl.loop(0, extra)
    def _(n):
        @pl.when(n >= slots.shape[0])
        def _():
            spill_out(spill, slots, sems, n - slots.shape[0]).wait()

        _, s, _, t = place(meta, rows[kept + n])
        kernel_values(xt, ya, s, t, sums, slots, lax.rem(n, slots.shape[0]))
        spill_out(spill, slots, sems, n).start()

    @pl.loop(jnp.maximum(extra - slots.shape[0], 0), extra)
    def _(n):
        spill_out(spill, slots, sems, n).wait()

    for s in range(blocks):
        total[:, s * BLK : (s + 1) * BLK] = lane_sums(sums[s])


def near_rows_kernel(meta, xt, y, own_total, keep, total, c, rows, ya, sums):
    fill_offsets(y, c)
    fill_targets(y, c, ya)
    sums[...] = jnp.zeros_like(sums)
    (count,) = list_rows(meta, (near_side(meta), rows))
    row_pairs(meta, rows, count, xt, ya, sums, keep, KEEP_NEAR)
    for s in range(sums.shape[0]):
        here = slice(s * BLK, (s + 1) * BLK)
        total[:, here] = own_total[:, here] + lane_sums(sums[s])


def settle_kernel(
    meta, xt, x, y_near, c_near, y_own, c_own, y_far, norm, near_total, keep_near, log_src,
    potential, send_near, send_far, u, weight, fits, no_far,
    rows_near, rows_far, potential_row, potential_sem, c_far, ya, keep, sums, totals,
    x_block, y_block, c_block, col_top, col_mass,
):
    blocks = u.shape[0]
    top, mass, column = sums.at[0], sums.at[1], sums.at[2]
    fill_offsets(y_far, c_far)
    fill_targets(y_far, c_far, ya)
    sums[...] = jnp.zeros_like(sums)
    near = near_side(meta)
    count_near, count_far = list_rows(meta, (near, rows_near), (-near, rows_far))
    row_pairs(meta, rows_far, count_far, xt, ya, sums, keep, KEEP_FAR)

    lowest = jnp.minimum(jnp.minimum(c_near[...], c_far[...]), c_own[...])
    x2 = jnp.max(norm[...], axis=1, keepdims=True)
    c_min = jnp.min(lowest, axis=1, keepdims=True)
    y2 = jnp.maximum(10.0 - c_min, 0.0)
    extent = x2 + 10.0 + 2.0 * jnp.sqrt(x2) * jnp.sqrt(y2) - c_min
    in_range = jnp.max(extent) <= SPAN
    alone = (meta[0] == 0) | (meta[0] == meta[2] - 1)
    no_far[...] = jnp.full_like(no_far, jnp.where(alone, FLOOR, 0.0))
    fits[...] = jnp.broadcast_to(jnp.where(extent <= SPAN, 1.0, 0.0), fits.shape)
    offset = lambda side, t: jnp.where(side == near, t, blocks + t)

    @pl.when(in_range)
    def _():
        index = lax.broadcasted_iota(jnp.int32, (8, BLK), 0)
        for s in range(blocks):
            here = slice(s * BLK, (s + 1) * BLK)
            total = near_total[:, here] + lane_sums(sums[s])
            w = log_src[:, here] - jnp.log(total)
            weight[:, here] = w
            value = jnp.exp(w)
            high = value.astype(bf16).astype(f32)
            u[s] = jnp.where(index == 0, high, jnp.where(index == 1, value - high, 0.0))
        potential_row[...] = 0.5 * (weight[...] + norm[...])
        hand_over = pltpu.make_async_copy(potential_row, potential, potential_sem)
        hand_over.start()
        totals[...] = jnp.zeros_like(totals)
        column_pairs(
            meta, rows_far, count_far, xt, ya, u, keep, KEEP_FAR,
            keep, KEEP_FAR, totals, blocks,
        )

        @pl.when(count_near > KEEP_NEAR)
        def _():
            refill_targets(y_near, c_near, ya)

        column_pairs(
            meta, rows_near, count_near, xt, ya, u, keep_near, KEEP_NEAR,
            keep, KEEP_FAR, totals, 0,
        )
        for t in range(blocks):
            here = slice(t * BLK, (t + 1) * BLK)
            send_near[:, here] = logs(jnp.sum(totals[t], axis=0, keepdims=True))
            send_far[:, here] = logs(jnp.sum(totals[blocks + t], axis=0, keepdims=True))
        hand_over.wait()

    @pl.when(jnp.logical_not(in_range))
    def _():
        ys = (y_near, y_own, y_far)
        cs = (c_near, c_own, c_far)
        general_rows(meta, x, ys, cs, x_block, y_block, c_block, top, mass, weight)
        weight[...] = log_src[...] - weight[...]
        u[...] = jnp.zeros_like(u)
        col_top[...] = jnp.full_like(col_top, FLOOR)
        col_mass[...] = jnp.zeros_like(col_mass)
        general_columns(
            meta, False, offset, x, ys, cs, x_block, y_block, c_block, weight, column,
            col_top, col_mass,
        )
        for t in range(blocks):
            here = slice(t * BLK, (t + 1) * BLK)
            send_near[:, here] = (col_top[t] + logs(col_mass[t]))[0:1, :]
            send_far[:, here] = (col_top[blocks + t] + logs(col_mass[blocks + t]))[0:1, :]
        potential_row[...] = 0.5 * (weight[...] + norm[...])
        pltpu.sync_copy(potential_row, potential)


def own_columns_kernel(
    meta, x, y, c, keep, spill, u, weight, fits,
    out,
    rows, slots, sems, totals, x_block, y_block, c_block, column, col_top, col_mass,
):
    blocks = u.shape[0]
    in_range = jnp.max(fits[...]) > 0.5
    (count,) = list_rows(meta, (0, rows))

    @pl.when(in_range)
    def _():
        kept = jnp.minimum(count, KEEP_OWN)
        extra = count - kept

        @pl.loop(0, jnp.minimum(extra, slots.shape[0]))
        def _(n):
            spill_in(spill, slots, sems, n).start()

        totals[...] = jnp.zeros_like(totals)
        column_pairs(meta, rows, kept, None, None, u, keep, KEEP_OWN, None, 0, totals, 0)

        @pl.loop(0, extra)
        def _(n):
            spill_in(spill, slots, sems, n).wait()
            _, s, _, t = place(meta, rows[kept + n])
            values = slots[lax.rem(n, slots.shape[0])]
            totals[t] += jnp.dot(u[s].astype(bf16), values, preferred_element_type=f32)

            @pl.when(n + slots.shape[0] < extra)
            def _():
                spill_in(spill, slots, sems, n + slots.shape[0]).start()

        for t in range(blocks):
            out[:, t * BLK : (t + 1) * BLK] = logs(jnp.sum(totals[t], axis=0, keepdims=True))

    @pl.when(jnp.logical_not(in_range))
    def _():
        col_top[...] = jnp.full_like(col_top, FLOOR)
        col_mass[...] = jnp.zeros_like(col_mass)
        general_columns(
            meta, True, lambda side, t: t, x, (None, y, None), (None, c, None),
            x_block, y_block, c_block, weight, column, col_top, col_mass,
        )
        for t in range(blocks):
            here = slice(t * BLK, (t + 1) * BLK)
            out[:, here] = (col_top[t] + logs(col_mass[t]))[0:1, :]


def call(kernel, operands, outs, scratch, limit, pairs, outside=(), outside_outs=()):
    in_vmem = pl.BlockSpec(memory_space=pltpu.VMEM)
    in_smem = pl.BlockSpec(memory_space=pltpu.SMEM)
    anywhere = pl.BlockSpec(memory_space=pl.ANY)
    return pl.pallas_call(
        kernel,
        out_shape=outs,
        in_specs=[in_smem]
        + [anywhere if n in outside else in_vmem for n in range(1, len(operands))],
        out_specs=tuple(
            anywhere if out in outside_outs else in_vmem for out in range(len(outs))
        ),
        scratch_shapes=scratch,
        compiler_params=pltpu.CompilerParams(vmem_limit_bytes=limit << 20),
        cost_estimate=pl.CostEstimate(
            flops=pairs * 2 * BLK * BLK * 256, bytes_accessed=1 << 20, transcendentals=pairs * BLK * BLK
        ),
    )(*operands)


def on_device(source_emb, target_emb, target_pot, log_src, log_tgt, pair_list):
    position = lax.axis_index(AXES)
    width = source_emb.shape[1]
    blocks = width // BLK
    row = jax.ShapeDtypeStruct((1, width), f32)
    pots = target_pot.reshape(width // 128, 128)
    pots = jnp.pad(pots, ((0, W - width // 128), (0, 0)))
    packed = jnp.concatenate([target_emb, pots], axis=1)
    from_near = swapped(packed, True)
    from_far = swapped(packed, False)
    twice = 2.0 * target_pot.astype(f32)

    mine = lax.dynamic_slice_in_dim(pair_list, position * P_DEV, MOST, 0)
    meta = jnp.concatenate(
        [jnp.stack([position, jnp.int32(blocks), jnp.int32(lax.axis_size(AXES))]).astype(jnp.int32), mine[:, 0], mine[:, 1]]
    )

    def kept(n):
        return pltpu.VMEM((n, BLK, BLK), bf16)

    sums_shape = (blocks, BLK, 128)
    ya_shape = pltpu.VMEM((blocks, DEPTH, BLK), bf16)
    rows_shape = pltpu.SMEM((MOST + 1,), jnp.int32)
    row_here = pltpu.VMEM((1, width), f32)
    xt, keep_own, spill, own_total, c_own, norm = call(
        own_rows_kernel,
        (meta, source_emb, packed),
        (pltpu.VMEM((blocks, BLK, DEPTH), bf16), kept(KEEP_OWN),
         jax.ShapeDtypeStruct((MOST - KEEP_OWN, BLK, BLK), bf16), row_here, row_here, row_here),
        [rows_shape, ya_shape, pltpu.VMEM(sums_shape, f32), kept(2), pltpu.SemaphoreType.DMA((2,))],
        LIMITS[0],
        9,
        (),
        (2,),
    )
    keep_near, near_total, c_near = call(
        near_rows_kernel,
        (meta, xt, from_near, own_total),
        (kept(KEEP_NEAR), row_here, row_here),
        [rows_shape, ya_shape, pltpu.VMEM(sums_shape, f32)],
        LIMITS[1],
        4,
    )
    block_scratch = [pltpu.VMEM((W, BLK), bf16)] * 2 + [pltpu.VMEM((1, BLK), f32)]
    wide = pltpu.VMEM((BLK, 128), f32)
    one = jax.ShapeDtypeStruct((1, 128), f32)
    potential, send_near, send_far, u, weight, fits, no_far = call(
        settle_kernel,
        (meta, xt, source_emb, from_near, c_near, target_emb, c_own, from_far, norm,
         near_total, keep_near, log_src.reshape(1, width)),
        (row, row, row, pltpu.VMEM((blocks, 8, BLK), f32), row, one, row_here),
        [rows_shape, rows_shape, row_here, pltpu.SemaphoreType.DMA, row_here, ya_shape, kept(KEEP_FAR + 1),
         pltpu.VMEM(sums_shape, f32), pltpu.VMEM((2 * blocks, 8, BLK), f32)] + block_scratch
        + [pltpu.VMEM((2 * blocks, 1, BLK), f32)] * 2,
        LIMITS[2],
        8,
        (2, 3, 5),
        (0,),
    )
    got_far = swapped(send_far, False)
    got_near = swapped(send_near, True)
    (own,) = call(
        own_columns_kernel,
        (meta, source_emb, target_emb, c_own, keep_own, spill, u, weight, fits),
        (row,),
        [rows_shape, kept(SLOTS), pltpu.SemaphoreType.DMA((SLOTS,)), pltpu.VMEM((blocks, 8, BLK), f32)] + block_scratch + [wide]
        + [pltpu.VMEM((blocks, 1, BLK), f32)] * 2,
        LIMITS[3],
        6,
        (1, 2, 5),
    )
    got_far = (got_far + no_far).reshape(width)
    got_near = got_near.reshape(width)
    own = own.reshape(width)
    top = jnp.maximum(jnp.maximum(got_far, got_near), own)
    total = jnp.exp(got_far - top) + jnp.exp(got_near - top) + jnp.exp(own - top)
    target_potential = 0.5 * (log_tgt + twice - (top + jnp.log(total)))
    return potential.reshape(width), target_potential


def solution(mesh):
    return jax.shard_map(
        on_device,
        mesh=mesh,
        in_specs=(P(None, AXES), P(None, AXES), P(AXES), P(AXES), P(AXES), P()),
        out_specs=(P(AXES), P(AXES)),
        check_vma=False,
    )
```
